256 devices in a mesh: dp: 32 (over x, z), seq: 8 (over y, core).
Axes of the slice: x: 4, y: 4, z: 8, core: 2. Of those that a mesh axis runs over, the one named last changes fastest.
Arguments:
- queries: bfloat16 [32768, 3072], P(('dp', 'seq')), may hold values from -150 to 150
- key_rows: bfloat16 [32768, 3072], P(('dp', 'seq')), may hold values from -5 to 5
- values: bfloat16 [32768, 3072], P(('dp', 'seq')), may hold values from -6 to 6
- target: bfloat16 [32768, 3072], P(('dp', 'seq')), may hold values from -18 to 18
- row_clip: int32 [32768], P(('dp', 'seq')), may hold values from -1 to 1, as said below
- ratios: float32 [32, 2], P('dp'), may hold values from 0.5 to 2
- ref_loss: float32 [32, 2], P('dp'), may hold values from 0.5 to 4
- noise_level: int32 [1], replicated, may hold values from 0 to 999
Outputs:
- grad_queries: bfloat16 [32768, 3072], P(('dp', 'seq'))
- grad_keys: bfloat16 [32768, 3072], P(('dp', 'seq'))
- grad_values: bfloat16 [32768, 3072], P(('dp', 'seq'))
- clip_loss: float32 [32, 2], P('dp')
The draws below stay inside these ranges and needn't reach their ends.
Inputs may be any that keep to these rules, and one draw needn't show every extreme that they name: `row_clip`: the rows a device sends to group g are rows g * 4 to (g+1) * 4 - 1 of its block, used rows first, at least two fifths of them used; every clip of every group has rows.
All inputs are finite; a program needn't handle non-finite values.
Results may differ from the reference program's by a relative error of at most 0.0058.
Values may be sent and summed in bfloat16 or wider, within the bound.
No kernel may reach another device: no remote copies, remote signals or barrier semaphores. Data moves between devices by JAX's collectives and lax.ppermute only.
A program may use at most 64 MiB of HBM per device.

```python
import math
import jax
import jax.numpy as jnp
from jax import lax

HEADS = 24
HD = 128
CLIPS_G = 2
LEVELS = 1000
TOK_DEV = 128
CAP = 4
ROWS = 32768
N_DP = 32
N_SEQ = 8


def shared_keys(key):
    base_key = jax.random.fold_in(key, 0)
    base = jnp.clip(jax.random.normal(base_key, (ROWS, HEADS * HD), jnp.float32), -5.0, 5.0)
    return base


def draw_key_rows(key, part):
    base = shared_keys(key)
    result = base
    return result.astype(jnp.bfloat16)


def draw_queries(key, part):
    key = jax.random.fold_in(key, 3)
    result = jnp.clip(jax.random.normal(key, (ROWS, HEADS * HD), jnp.float32), -5.0, 5.0)
    return result.astype(jnp.bfloat16)


def draw_target(key, part):
    key = jax.random.fold_in(key, 9)
    head_index = (jnp.arange(HEADS * HD, dtype=jnp.int32) // HD).astype(jnp.float32)
    rising = head_index[None, :] / (HEADS - 1)
    result = jnp.clip(jax.random.normal(key, (ROWS, HEADS * HD), jnp.float32), -6.0, 6.0) * jnp.exp(rising * math.log(3.0))
    return result.astype(jnp.bfloat16)


def draw_row_clip(key, part):
    key = jax.random.fold_in(key, 5)
    devices = N_DP * N_SEQ
    positions_all = devices * CAP
    key_counts, key_first = jax.random.split(key, 2)
    fewest = (2 * CAP + 4) // 5
    counts = jax.random.randint(key_counts, (devices, N_DP, 1), fewest, CAP + 1)
    slot_row = jnp.arange(CAP, dtype=jnp.int32)[None, None, :]
    position = jnp.arange(devices, dtype=jnp.int32)[:, None, None] * CAP + slot_row
    first_cut = jax.random.randint(key_first, (1, N_DP, 1), positions_all // 4, positions_all - positions_all // 4)
    clip_index = (position >= first_cut).astype(jnp.int32)
    return jnp.where(slot_row < counts, clip_index, -1).reshape(devices * N_DP * CAP)


def shard_levels(stream_key, extent, cuts, low, high):
    gain = 1.0
    for dim, shards_of in cuts:
        steps = jax.random.uniform(jax.random.fold_in(jax.random.fold_in(stream_key, 6), dim), (shards_of,), jnp.float32, low / len(cuts), high / len(cuts))
        gain = gain * jnp.repeat(jnp.exp(steps), extent[dim] // shards_of).reshape((-1,) + (1,) * (len(extent) - 1 - dim))
    return gain


def bell_draw(stream_key, shape, scale, reach, pieces=(), kind=jnp.bfloat16):
    loudness = shard_levels(stream_key, shape, pieces, -0.22, 0.18) if pieces else 1.0
    values = jax.random.normal(stream_key, shape, jnp.float32) * scale * loudness
    return jnp.minimum(jnp.maximum(values, -reach), reach).astype(kind)


def setup_inputs(seed: int = 0) -> dict:
    seeds = jax.random.split(jax.random.key(seed), 9)
    return {
        "queries": draw_queries(jax.random.fold_in(seeds[8], 71), 0),
        "key_rows": draw_key_rows(jax.random.fold_in(seeds[8], 71), 0),
        "values": bell_draw(seeds[2], (ROWS, HEADS * HD), 1.0, 6.0, ((0, 256),)),
        "target": draw_target(jax.random.fold_in(seeds[8], 71), 0),
        "row_clip": draw_row_clip(jax.random.fold_in(seeds[8], 71), 0),
        "ratios": jnp.clip(jnp.exp(math.log(2.0) - 1.3862944 * jax.random.uniform(seeds[5], (N_DP, CLIPS_G), jnp.float32) ** shard_levels(seeds[5], (N_DP, CLIPS_G), ((0, 32),), -0.2, 0.2)), 0.5, 2.0),
        "ref_loss": jnp.clip(jnp.exp(math.log(4.0) - 2.0794415 * jax.random.uniform(seeds[6], (N_DP, CLIPS_G), jnp.float32) ** shard_levels(seeds[6], (N_DP, CLIPS_G), ((0, 32),), -0.2, 0.2)), 0.5, 4.0),
        "noise_level": jax.random.randint(seeds[7], (1,), 0, LEVELS).astype(jnp.int32),
    }


NEG_FILL = -1.0e30
SHIFT_FACTOR = 5.0
LOSS_SCALE = 2.0 ** 21


def level_weight(noise_level):
    fraction = 1.0 - noise_level[0].astype(jnp.float32) / LEVELS
    sigma = SHIFT_FACTOR * fraction / (1.0 + (SHIFT_FACTOR - 1.0) * fraction)
    return 1.0 / (sigma * sigma + (1.0 - sigma) * (1.0 - sigma))


def to_groups(array):
    rest = array.shape[1:]
    shaped = array.reshape((N_DP * N_SEQ, N_DP, CAP) + rest)
    shaped = jnp.swapaxes(shaped, 0, 1)
    return shaped.reshape((N_DP, N_DP * N_SEQ * CAP) + rest)


def from_groups(array):
    rest = array.shape[2:]
    shaped = array.reshape((N_DP, N_DP * N_SEQ, CAP) + rest)
    shaped = jnp.swapaxes(shaped, 0, 1)
    return shaped.reshape((N_DP * N_SEQ * TOK_DEV,) + rest)


def head_probs(query_head, key_head, allowed):
    scores = jnp.dot(query_head, key_head.T, preferred_element_type=jnp.float32) * (HD ** -0.5)
    scores = jnp.where(allowed, scores, NEG_FILL)
    largest = jnp.max(scores, axis=1, keepdims=True)
    expo = jnp.exp(scores - largest)
    return expo / jnp.sum(expo, axis=1, keepdims=True)


def head_forward(query_head, key_head, value_head, allowed):
    probs = head_probs(query_head, key_head, allowed)
    return jnp.dot(probs.astype(jnp.bfloat16), value_head, preferred_element_type=jnp.float32)


def head_backward(query_head, key_head, value_head, grad_head, allowed):
    probs = head_probs(query_head, key_head, allowed)
    probs_low = probs.astype(jnp.bfloat16)
    grad_probs = jnp.dot(grad_head, value_head.T, preferred_element_type=jnp.float32)
    grad_value = jnp.dot(probs_low.T, grad_head, preferred_element_type=jnp.float32)
    inner = jnp.sum(probs * grad_probs, axis=1, keepdims=True)
    grad_scores = (probs * (grad_probs - inner)).astype(jnp.bfloat16)
    grad_query = jnp.dot(grad_scores, key_head, preferred_element_type=jnp.float32) * (HD ** -0.5)
    grad_key = jnp.dot(grad_scores.T, query_head, preferred_element_type=jnp.float32) * (HD ** -0.5)
    return grad_query.astype(jnp.bfloat16), grad_key.astype(jnp.bfloat16), grad_value.astype(jnp.bfloat16)


def split_heads(array):
    return jnp.swapaxes(array.reshape(array.shape[0], HEADS, HD), 0, 1)


def join_heads(array):
    return jnp.swapaxes(array, 0, 1).reshape(array.shape[1], HEADS * HD)


def group_pass(query_group, key_group, value_group, target_group, clip_group, ratio_group, ref_group, weight_level):
    allowed = (clip_group[:, None] == clip_group[None, :]) & (clip_group[None, :] >= 0)
    query_heads = split_heads(query_group)
    key_heads = split_heads(key_group)
    value_heads = split_heads(value_group)

    def forward_one(trio):
        return head_forward(trio[0], trio[1], trio[2], allowed)

    output = lax.map(forward_one, (query_heads, key_heads, value_heads))
    error = output - split_heads(target_group).astype(jnp.float32)
    row_squares = jnp.sum(error * error, axis=(0, 2))
    onehot = (clip_group[:, None] == jnp.arange(CLIPS_G, dtype=jnp.int32)[None, :]).astype(jnp.float32)
    sums = jnp.sum(onehot * row_squares[:, None], axis=0)
    counts = jnp.sum(onehot, axis=0)
    width = HEADS * HD
    loss = weight_level * sums / (counts * width)
    weight = ratio_group * loss / ref_group
    coef = weight_level * weight * 2.0 * LOSS_SCALE / (counts * width)
    coef_row = jnp.sum(onehot * coef[None, :], axis=1)
    grad_out = (coef_row[None, :, None] * error).astype(jnp.bfloat16)

    def backward_one(quad):
        return head_backward(quad[0], quad[1], quad[2], quad[3], allowed)

    grad_q, grad_k, grad_v = lax.map(backward_one, (query_heads, key_heads, value_heads, grad_out))
    return join_heads(grad_q), join_heads(grad_k), join_heads(grad_v), loss


def reference(queries, key_rows, values, target, row_clip, ratios, ref_loss, noise_level):
    weight_level = level_weight(noise_level)
    grouped = (to_groups(queries), to_groups(key_rows), to_groups(values), to_groups(target), to_groups(row_clip), ratios, ref_loss)

    def one_group(items):
        return group_pass(items[0], items[1], items[2], items[3], items[4], items[5], items[6], weight_level)

    grad_q, grad_k, grad_v, loss = lax.map(one_group, grouped)
    return from_groups(grad_q), from_groups(grad_k), from_groups(grad_v), loss
```

```python
import functools

import jax
import jax.numpy as jnp
from jax import lax
from jax.experimental import pallas as pl
from jax.experimental.pallas import tpu as pltpu
from jax.sharding import PartitionSpec as P

HEADS = 24
HD = 128
CLIPS_G = 2
LEVELS = 1000

SHIFT_FACTOR = 5.0
LOSS_SCALE = 2.0**21
MASK_FILL = 1e30
LOG2E = 1.4426950408889634
WIDTH = HEADS * HD

CAP = 4
IN_PIECES = 13
OUT_PIECES = 10
BLOCK = 256


def level_weight(noise_level):
    fraction = 1.0 - noise_level[0].astype(jnp.float32) / LEVELS
    sigma = SHIFT_FACTOR * fraction / (1.0 + (SHIFT_FACTOR - 1.0) * fraction)
    return 1.0 / (sigma * sigma + (1.0 - sigma) * (1.0 - sigma))


def low_half(shape=(8, HD)):
    return lax.broadcasted_iota(jnp.int32, shape, 0) % 8 < CAP


def swap(tile):
    return pltpu.roll(tile, CAP, 0)


def pack_kernel(q_ref, k_ref, v_ref, t_ref, clip_ref, out_ref):
    low = low_half()
    tensors = [ref[...].astype(jnp.float32) for ref in (q_ref, k_ref, v_ref, t_ref)]
    step = pl.program_id(0)
    rows = q_ref.shape[0]
    pick = lax.broadcasted_iota(jnp.int32, (rows, HD), 0) + step * rows
    lane = lax.broadcasted_iota(jnp.int32, (rows, HD), 1)
    labels = jnp.sum(
        jnp.where(pick == lane, jnp.broadcast_to(clip_ref[...].astype(jnp.float32), (rows, HD)), 0.0),
        axis=1,
        keepdims=True,
    )
    labels = jnp.broadcast_to(labels, (rows, HD))
    seq_size = tensors[0].shape[1] // (3 * HD)
    for tile in range(rows // 8):
        at = slice(tile * 8, tile * 8 + 8)
        label_tile = labels[at]
        for half in range(2):
            made = []
            for dest in range(seq_size):
                pieces = []
                for head in range(3):
                    col = (dest * 3 + head) * HD
                    for tensor in tensors:
                        pieces.append(tensor[at, col : col + HD])
                pieces.append(label_tile)
                made.extend(pieces)
            tiles = []
            for first, second in zip(made[::2], made[1::2]):
                if half == 0:
                    tiles.append(jnp.where(low, first, swap(second)))
                else:
                    tiles.append(jnp.where(low, swap(first), second))
            count = 8 * len(tiles)
            start = (tile * 2 + half) * count
            out_ref[start : start + count, :] = jnp.concatenate(tiles, axis=0).astype(jnp.bfloat16)


def pack(queries, key_rows, values, target, clip_row):
    tok_rows, width = queries.shape
    steps = 4
    rows = tok_rows // steps
    spec = pl.BlockSpec((rows, width), lambda i: (i, 0))
    out_rows = tok_rows // CAP * (width // (3 * HD)) * IN_PIECES * CAP
    return pl.pallas_call(
        pack_kernel,
        grid=(steps,),
        in_specs=[spec] * 4 + [pl.BlockSpec((1, tok_rows), lambda i: (0, 0))],
        out_specs=pl.BlockSpec((out_rows // steps, HD), lambda i: (i, 0)),
        out_shape=jax.ShapeDtypeStruct((out_rows, HD), jnp.bfloat16),
        compiler_params=pltpu.CompilerParams(vmem_limit_bytes=40 * 2**20),
        name="pack",
    )(queries, key_rows, values, target, clip_row)


def split3(value):
    high = value.astype(jnp.bfloat16).astype(jnp.float32)
    rest = value - high
    mid = rest.astype(jnp.bfloat16).astype(jnp.float32)
    return high, mid, rest - mid


def nt_dot(a, b):
    return lax.dot_general(a, b, (((1,), (1,)), ((), ())), preferred_element_type=jnp.float32)


def tn_dot(a, b):
    return lax.dot_general(a, b, (((0,), (0,)), ((), ())), preferred_element_type=jnp.float32)


def attend_kernel(in_ref, factor_ref, out_ref, x_ref, lab_ref, fq_ref, fk_ref, g_ref):
    low = low_half()
    total = x_ref.shape[1]
    pair = 2 * IN_PIECES * CAP

    def sort_in(i, carry):
        base = pl.multiple_of(i * (2 * pair), 2 * pair)
        block = in_ref[pl.ds(base, 2 * pair), :].astype(jnp.float32)
        at = pl.ds(pl.multiple_of(i * 16, 16), 16)
        for j in range(IN_PIECES):
            halves = []
            for u in range(2):
                a, b = j // 2, (IN_PIECES + j) // 2
                lo = block[u * pair + a * 8 : u * pair + a * 8 + 8]
                hi = block[u * pair + b * 8 : u * pair + b * 8 + 8]
                if j % 2 == 0:
                    halves.append(jnp.where(low, lo, hi))
                else:
                    halves.append(swap(jnp.where(low, hi, lo)))
            both = jnp.concatenate(halves, axis=0)
            if j < IN_PIECES - 1:
                x_ref[j, at, :] = both.astype(jnp.bfloat16)
            else:
                lab_ref[at, :] = both
        return carry

    lax.fori_loop(0, total // 16, sort_in, 0, unroll=4)

    label = lab_ref[...]
    lane = lax.broadcasted_iota(jnp.int32, (total, HD), 1)
    is0 = jnp.where(label == 0.0, 1.0, 0.0)
    is1 = jnp.where(label == 1.0, 1.0, 0.0)
    empty = jnp.where(label < 0.0, 1.0, 0.0)
    fk_ref[...] = jnp.where(
        lane == 0, is0, jnp.where(lane == 1, is1, jnp.where(lane == 2, empty, 0.0))
    ).astype(jnp.bfloat16)
    fq_ref[...] = jnp.where(
        lane == 0,
        (is0 - 1.0) * MASK_FILL,
        jnp.where(lane == 1, (is1 - 1.0) * MASK_FILL, jnp.where(lane == 2, -MASK_FILL, 0.0)),
    ).astype(jnp.bfloat16)
    counts = (jnp.sum(is0, axis=0, keepdims=True), jnp.sum(is1, axis=0, keepdims=True))

    scale = HD**-0.5

    def one_head(head, sums):
        s0, s1 = sums
        key = x_ref[head * 4 + 1]
        value = x_ref[head * 4 + 2]
        key_wide = jnp.concatenate([key, fk_ref[...]], axis=1)
        for block in range(total // BLOCK):
            at = slice(block * BLOCK, (block + 1) * BLOCK)
            query = x_ref[head * 4, at, :]
            query_wide = jnp.concatenate([query, fq_ref[at, :]], axis=1)
            scores = nt_dot(query_wide, key_wide)
            largest = jnp.max(scores, axis=1, keepdims=True)
            expo = jnp.exp2((scores - largest) * (scale * LOG2E))
            probs = expo * (1.0 / jnp.sum(expo, axis=1, keepdims=True))
            probs_low = probs.astype(jnp.bfloat16)
            output = jnp.dot(probs_low, value, preferred_element_type=jnp.float32)
            error = output - x_ref[head * 4 + 3, at, :].astype(jnp.float32)
            lab = lab_ref[at, :]
            error = jnp.where(lab >= 0.0, error, 0.0)
            square = error * error
            s0 = s0 + jnp.sum(jnp.where(lab == 0.0, square, 0.0), axis=0, keepdims=True)
            s1 = s1 + jnp.sum(jnp.where(lab == 1.0, square, 0.0), axis=0, keepdims=True)
            grad_low = error.astype(jnp.bfloat16)
            grad_probs = nt_dot(grad_low, value)
            inner = jnp.sum(probs * grad_probs, axis=1, keepdims=True)
            grad_scores = (probs * (grad_probs - inner)).astype(jnp.bfloat16)
            g_ref[head * 3, at, :] = jnp.dot(grad_scores, key, preferred_element_type=jnp.float32) * scale
            grad_key = tn_dot(grad_scores, query) * scale
            grad_value = tn_dot(probs_low, grad_low)
            if block == 0:
                g_ref[head * 3 + 1] = grad_key
                g_ref[head * 3 + 2] = grad_value
            else:
                g_ref[head * 3 + 1] += grad_key
                g_ref[head * 3 + 2] += grad_value
        return s0, s1

    zero = jnp.zeros((1, HD), jnp.float32)
    s0, s1 = lax.fori_loop(0, 3, one_head, (zero, zero))

    parts = []
    for clip, (acc, count) in enumerate(zip((s0, s1), counts)):
        both = factor_ref[:, :HD] / (count * WIDTH)
        loss = jnp.sum(acc, axis=1, keepdims=True) * both
        parts.append((loss, loss * factor_ref[:, (1 + clip) * HD : (2 + clip) * HD] * both))
    lane_row = lax.broadcasted_iota(jnp.int32, (1, HD), 1)

    def spread(value, first):
        high, mid, rest = split3(value)
        return jnp.where(
            lane_row == first,
            high,
            jnp.where(lane_row == first + 1, mid, jnp.where(lane_row == first + 2, rest, 0.0)),
        )

    losses = spread(parts[0][0], 3) + spread(parts[1][0], 6)
    extra0 = losses + spread(parts[0][1], 0)
    extra1 = losses + spread(parts[1][1], 0)
    out_pair = 2 * OUT_PIECES * CAP

    def sort_out(i, carry):
        at = pl.ds(pl.multiple_of(i * 8, 8), 8)
        lab = lab_ref[at, :]
        tiles = [g_ref[j, at, :] for j in range(OUT_PIECES - 1)]
        tiles.append(jnp.where(lab == 0.0, extra0, jnp.where(lab == 1.0, extra1, losses)))
        turned = [swap(tile) for tile in tiles]
        first = [jnp.where(low, tiles[j], turned[j + 1]) for j in range(0, OUT_PIECES, 2)]
        second = [jnp.where(low, turned[j], tiles[j + 1]) for j in range(0, OUT_PIECES, 2)]
        base = pl.multiple_of(i * out_pair, out_pair)
        out_ref[pl.ds(base, out_pair), :] = jnp.concatenate(first + second, axis=0).astype(jnp.bfloat16)
        return carry

    lax.fori_loop(0, total // 8, sort_out, 0, unroll=4)


def attend(arrived, factors, sources):
    total = sources * CAP
    whole = pl.BlockSpec(memory_space=pltpu.VMEM)
    return pl.pallas_call(
        attend_kernel,
        in_specs=[whole, whole],
        out_specs=whole,
        out_shape=jax.ShapeDtypeStruct((sources * OUT_PIECES * CAP, HD), jnp.bfloat16),
        scratch_shapes=[
            pltpu.VMEM((12, total, HD), jnp.bfloat16),
            pltpu.VMEM((total, HD), jnp.float32),
            pltpu.VMEM((total, HD), jnp.bfloat16),
            pltpu.VMEM((total, HD), jnp.bfloat16),
            pltpu.VMEM((9, total, HD), jnp.float32),
        ],
        compiler_params=pltpu.CompilerParams(vmem_limit_bytes=50 * 2**20),
        name="attend",
    )(arrived, factors)


def unpack_kernel(here_ref, in_ref, dq_ref, dk_ref, dv_ref, loss_ref, *, seq_size):
    low = low_half()
    lane = lax.broadcasted_iota(jnp.int32, (8, HD), 1)
    rows = dq_ref.shape[0]
    chunk = OUT_PIECES * CAP
    step = pl.program_id(0)
    outs = (dq_ref, dk_ref, dv_ref)
    block = in_ref[...].astype(jnp.float32)

    def piece(tile, dest, j):
        even = ((tile * 2) * seq_size + dest) * chunk + (j // 2) * 8
        odd = ((tile * 2 + 1) * seq_size + dest) * chunk + (j // 2) * 8
        a, b = block[even : even + 8], block[odd : odd + 8]
        if j % 2 == 0:
            return jnp.where(low, a, swap(b))
        return jnp.where(low, swap(a), b)

    for two in range(rows // 16):
        coefs = []
        for tile in (two * 2, two * 2 + 1):
            extra = piece(tile, 0, OUT_PIECES - 1)
            for dest in range(1, seq_size):
                extra = extra + piece(tile, dest, OUT_PIECES - 1)
            coef = jnp.sum(jnp.where(lane < 3, extra, 0.0), axis=1, keepdims=True)
            coefs.append(jnp.broadcast_to(coef, (8, HD)))
            for half in range(2):
                group = step * (rows // CAP) + tile * 2 + half

                @pl.when(group == here_ref[0])
                def _():
                    line = extra[half * CAP : half * CAP + 1]
                    lane_row = lax.broadcasted_iota(jnp.int32, (1, HD), 1)
                    for clip in range(CLIPS_G):
                        mine = (lane_row >= 3 + 3 * clip) & (lane_row < 6 + 3 * clip)
                        loss_ref[0:1, clip : clip + 1] = jnp.sum(
                            jnp.where(mine, line, 0.0), axis=1, keepdims=True
                        )

        for dest in range(seq_size):
            for head in range(3):
                col = (dest * 3 + head) * HD
                for index, ref in enumerate(outs):
                    both = [
                        piece(two * 2 + n, dest, head * 3 + index) * coefs[n] for n in range(2)
                    ]
                    ref[two * 16 : two * 16 + 16, col : col + HD] = jnp.concatenate(
                        both, axis=0
                    ).astype(jnp.bfloat16)


def unpack(returned, here, tok_rows, seq_size):
    steps = 4
    rows = tok_rows // steps
    width = seq_size * 3 * HD
    grad_spec = pl.BlockSpec((rows, width), lambda i: (i, 0))
    grad_shape = jax.ShapeDtypeStruct((tok_rows, width), jnp.bfloat16)
    return pl.pallas_call(
        functools.partial(unpack_kernel, seq_size=seq_size),
        grid=(steps,),
        in_specs=[
            pl.BlockSpec(memory_space=pltpu.SMEM),
            pl.BlockSpec((returned.shape[0] // steps, HD), lambda i: (i, 0)),
        ],
        out_specs=[grad_spec] * 3 + [pl.BlockSpec((1, CLIPS_G), lambda i: (0, 0))],
        out_shape=[grad_shape] * 3 + [jax.ShapeDtypeStruct((1, CLIPS_G), jnp.float32)],
        compiler_params=pltpu.CompilerParams(vmem_limit_bytes=40 * 2**20),
        name="unpack",
    )(here, returned)


def shards(queries, key_rows, values, target, row_clip, ratios, ref_loss, noise_level):
    seq_size = lax.axis_size("seq")
    devices = lax.axis_size("dp") * seq_size
    tok_rows = queries.shape[0]
    sent = pack(queries, key_rows, values, target, row_clip.reshape(1, tok_rows))
    sent = sent.reshape(devices * IN_PIECES, CAP, HD)
    arrived = lax.all_to_all(sent, ("dp", "seq"), split_axis=0, concat_axis=0, tiled=True)
    arrived = arrived.reshape(devices * IN_PIECES * CAP, HD)
    weight_level = level_weight(noise_level)
    step = ratios / ref_loss * (2.0 * LOSS_SCALE)
    factors = jnp.concatenate(
        [jnp.broadcast_to(weight_level, (1, HD))]
        + [jnp.broadcast_to(step[:, c : c + 1], (1, HD)) for c in range(CLIPS_G)],
        axis=1,
    )
    grads = attend(arrived, factors, devices)
    grads = grads.reshape(devices, OUT_PIECES * CAP, HD)
    returned = lax.all_to_all(grads, ("dp", "seq"), split_axis=0, concat_axis=0, tiled=True)
    returned = returned.reshape(devices * OUT_PIECES * CAP, HD)
    here = lax.axis_index("dp").reshape(1).astype(jnp.int32)
    return tuple(unpack(returned, here, tok_rows, seq_size))


def solution(mesh):
    placed = (
        P(("dp", "seq"), None),
        P(("dp", "seq"), None),
        P(("dp", "seq"), None),
        P(("dp", "seq"), None),
        P(("dp", "seq")),
        P("dp", None),
        P("dp", None),
        P(),
    )
    return jax.shard_map(
        shards,
        mesh=mesh,
        in_specs=placed,
        out_specs=(
            P(("dp", "seq"), None),
            P(("dp", "seq"), None),
            P(("dp", "seq"), None),
            P("dp", None),
        ),
        check_vma=False,
    )
```

```python
import functools

import jax
import jax.numpy as jnp
from jax import lax
from jax.experimental import pallas as pl
from jax.experimental.pallas import tpu as pltpu
from jax.sharding import PartitionSpec as P

HEADS = 24
HD = 128
CLIPS_G = 2
LEVELS = 1000

SHIFT_FACTOR = 5.0
LOSS_SCALE = 2.0**21
MASK_FILL = 1e30
LOG2E = 1.4426950408889634
WIDTH = HEADS * HD

CAP = 4
IN_PIECES = 13
OUT_PIECES = 10
BLOCK = 512
STRIP = 32
NCUT = 256
PARTS = 8
VMEM_LIMIT = 40 * 2**20
PACK_LIMIT = 61 * 2**20


def level_weight(noise_level):
    fraction = 1.0 - noise_level[0].astype(jnp.float32) / LEVELS
    sigma = SHIFT_FACTOR * fraction / (1.0 + (SHIFT_FACTOR - 1.0) * fraction)
    return 1.0 / (sigma * sigma + (1.0 - sigma) * (1.0 - sigma))


def low_half(shape=(8, HD)):
    return lax.broadcasted_iota(jnp.int32, shape, 0) % 8 < CAP


def swap(tile):
    return pltpu.roll(tile, CAP, 0)


def pack_kernel(q_ref, k_ref, v_ref, t_ref, clip_ref, out_ref, x_ref, c_ref, lab_ref, o_ref, in_sem, clip_sem, out_sem):
    low = low_half()
    tok_rows, width = q_ref.shape
    seq_size = width // (3 * HD)
    chunks = tok_rows // 16
    out_rows = o_ref.shape[0] // chunks

    def fetch(chunk, tensor):
        at = pl.ds(chunk * 16, 16)
        ref = (q_ref, k_ref, v_ref, t_ref)[tensor]
        return pltpu.make_async_copy(ref.at[at], x_ref.at[tensor, at], in_sem.at[chunk, tensor])

    def emit(chunk):
        at = pl.ds(chunk * out_rows, out_rows)
        return pltpu.make_async_copy(o_ref.at[at], out_ref.at[at], out_sem.at[chunk])

    clip_copy = pltpu.make_async_copy(clip_ref, c_ref, clip_sem.at[0])
    clip_copy.start()
    for chunk in range(chunks):
        for tensor in range(4):
            fetch(chunk, tensor).start()
    clip_copy.wait()
    row = lax.broadcasted_iota(jnp.int32, (tok_rows, tok_rows), 0)
    lane = lax.broadcasted_iota(jnp.int32, (tok_rows, tok_rows), 1)
    clips = jnp.broadcast_to(c_ref[...].astype(jnp.float32), (tok_rows, tok_rows))
    labels = jnp.sum(jnp.where(row == lane, clips, 0.0), axis=1, keepdims=True)
    lab_ref[...] = jnp.broadcast_to(labels, (tok_rows, HD))
    for chunk in range(chunks):
        for tensor in range(4):
            fetch(chunk, tensor).wait()
        at = slice(chunk * 16, chunk * 16 + 16)
        tensors = [x_ref[tensor, at, :].astype(jnp.float32) for tensor in range(4)]
        for tile in range(2):
            eight = slice(tile * 8, tile * 8 + 8)
            label_tile = lab_ref[chunk * 16 + tile * 8 : chunk * 16 + tile * 8 + 8, :]
            for half in range(2):
                made = []
                for dest in range(seq_size):
                    for head in range(3):
                        col = (dest * 3 + head) * HD
                        made.extend(tensor[eight, col : col + HD] for tensor in tensors)
                    made.append(label_tile)
                tiles = []
                for first, second in zip(made[::2], made[1::2]):
                    if half == 0:
                        tiles.append(jnp.where(low, first, swap(second)))
                    else:
                        tiles.append(jnp.where(low, swap(first), second))
                count = 8 * len(tiles)
                start = ((chunk * 2 + tile) * 2 + half) * count
                o_ref[start : start + count, :] = jnp.concatenate(tiles, axis=0).astype(jnp.bfloat16)
        emit(chunk).start()
    for chunk in range(chunks):
        emit(chunk).wait()


def pack(queries, key_rows, values, target, clip_row):
    tok_rows, width = queries.shape
    chunks = tok_rows // 16
    out_rows = tok_rows // CAP * (width // (3 * HD)) * IN_PIECES * CAP
    return pl.pallas_call(
        pack_kernel,
        in_specs=[pl.BlockSpec(memory_space=pltpu.HBM)] * 5,
        out_specs=pl.BlockSpec(memory_space=pltpu.HBM),
        out_shape=jax.ShapeDtypeStruct((out_rows, HD), jnp.bfloat16),
        scratch_shapes=[
            pltpu.VMEM((4, tok_rows, width), jnp.bfloat16),
            pltpu.VMEM((1, tok_rows), jnp.int32),
            pltpu.VMEM((tok_rows, HD), jnp.float32),
            pltpu.VMEM((out_rows, HD), jnp.bfloat16),
            pltpu.SemaphoreType.DMA((chunks, 4)),
            pltpu.SemaphoreType.DMA((1,)),
            pltpu.SemaphoreType.DMA((chunks,)),
        ],
        compiler_params=pltpu.CompilerParams(vmem_limit_bytes=PACK_LIMIT),
        name="pack",
    )(queries, key_rows, values, target, clip_row)


def split3(value):
    high = value.astype(jnp.bfloat16).astype(jnp.float32)
    rest = value - high
    mid = rest.astype(jnp.bfloat16).astype(jnp.float32)
    return high, mid, rest - mid


def nt_dot(a, b):
    return lax.dot_general(a, b, (((1,), (1,)), ((), ())), preferred_element_type=jnp.float32)


def tn_dot(a, b):
    return lax.dot_general(a, b, (((0,), (0,)), ((), ())), preferred_element_type=jnp.float32)


def attend_kernel(
    in_ref, factor_ref, sent_ref, out_ref, x_ref, lab_ref, fq_ref, fk_ref, g_ref,
    s_ref, p_ref, dp_ref, pl_ref, ds_ref, e_ref, out_sem,
):
    low = low_half()
    total = x_ref.shape[1]
    pair = 2 * IN_PIECES * CAP
    out_part = out_ref.shape[0] // PARTS

    def emit(part):
        at = pl.ds(part * out_part, out_part)
        return pltpu.make_async_copy(out_ref.at[at], sent_ref.at[at], out_sem.at[part])


    def sort_in(i, carry):
        base = pl.multiple_of(i * (2 * pair), 2 * pair)
        block = in_ref[pl.ds(base, 2 * pair), :].astype(jnp.float32)
        at = pl.ds(pl.multiple_of(i * 16, 16), 16)
        for j in range(IN_PIECES):
            halves = []
            for u in range(2):
                a, b = j // 2, (IN_PIECES + j) // 2
                lo = block[u * pair + a * 8 : u * pair + a * 8 + 8]
                hi = block[u * pair + b * 8 : u * pair + b * 8 + 8]
                if j % 2 == 0:
                    halves.append(jnp.where(low, lo, hi))
                else:
                    halves.append(swap(jnp.where(low, hi, lo)))
            both = jnp.concatenate(halves, axis=0)
            if j < IN_PIECES - 1:
                x_ref[j, at, :] = both.astype(jnp.bfloat16)
            else:
                lab_ref[at, :] = both
        return carry

    lax.fori_loop(0, total // 16, sort_in, 0, unroll=8)

    label = lab_ref[...]
    lane = lax.broadcasted_iota(jnp.int32, (total, HD), 1)
    is0 = jnp.where(label == 0.0, 1.0, 0.0)
    is1 = jnp.where(label == 1.0, 1.0, 0.0)
    empty = jnp.where(label < 0.0, 1.0, 0.0)
    fk_ref[...] = jnp.where(
        lane == 0, is0, jnp.where(lane == 1, is1, jnp.where(lane == 2, empty, 0.0))
    ).astype(jnp.bfloat16)
    fq_ref[...] = jnp.where(
        lane == 0,
        (is0 - 1.0) * MASK_FILL,
        jnp.where(lane == 1, (is1 - 1.0) * MASK_FILL, jnp.where(lane == 2, -MASK_FILL, 0.0)),
    ).astype(jnp.bfloat16)
    counts = (jnp.sum(is0, axis=0, keepdims=True), jnp.sum(is1, axis=0, keepdims=True))

    scale = HD**-0.5

    steps = [(head, block) for head in range(3) for block in range(total // BLOCK)]

    def rows_of(step):
        return slice(steps[step][1] * BLOCK, (steps[step][1] + 1) * BLOCK)

    def score_parts(step):
        head, at, slot = steps[step][0], rows_of(step), step % 2

        def part(n):
            cols = slice(n, n + NCUT)
            key_wide = jnp.concatenate([x_ref[head * 4 + 1, cols, :], fk_ref[cols, :]], axis=1)
            query_wide = jnp.concatenate([x_ref[head * 4, at, :], fq_ref[at, :]], axis=1)
            s_ref[slot, :, cols] = nt_dot(query_wide, key_wide)

        return [functools.partial(part, n) for n in range(0, total, NCUT)]

    def soft_parts(step):
        slot = step % 2

        def part(r):
            rows = slice(r, r + STRIP)
            scores = s_ref[slot, rows, :]
            largest = jnp.max(scores, axis=1, keepdims=True)
            expo = jnp.exp2((scores - largest) * (scale * LOG2E))
            probs = expo * (1.0 / jnp.sum(expo, axis=1, keepdims=True))
            p_ref[slot, rows, :] = probs
            pl_ref[slot, rows, :] = probs.astype(jnp.bfloat16)

        return [functools.partial(part, r) for r in range(0, BLOCK, STRIP)]

    def error_part(step, sums):
        head, at, slot = steps[step][0], rows_of(step), step % 2
        s0, s1 = sums
        output = jnp.dot(pl_ref[slot], x_ref[head * 4 + 2], preferred_element_type=jnp.float32)
        error = output - x_ref[head * 4 + 3, at, :].astype(jnp.float32)
        lab = lab_ref[at, :]
        error = jnp.where(lab >= 0.0, error, 0.0)
        square = error * error
        s0 = s0 + jnp.sum(jnp.where(lab == 0.0, square, 0.0), axis=0, keepdims=True)
        s1 = s1 + jnp.sum(jnp.where(lab == 1.0, square, 0.0), axis=0, keepdims=True)
        e_ref[slot] = error.astype(jnp.bfloat16)
        return s0, s1

    def grad_prob_parts(step):
        head, slot = steps[step][0], step % 2

        def part(n):
            cols = slice(n, n + NCUT)
            dp_ref[slot, :, cols] = nt_dot(e_ref[slot], x_ref[head * 4 + 2, cols, :])

        return [functools.partial(part, n) for n in range(0, total, NCUT)]

    def grad_score_parts(step):
        slot = step % 2

        def part(r):
            rows = slice(r, r + STRIP)
            grad_probs = dp_ref[slot, rows, :]
            probs = p_ref[slot, rows, :]
            inner = jnp.sum(probs * grad_probs, axis=1, keepdims=True)
            ds_ref[slot, rows, :] = (probs * (grad_probs - inner)).astype(jnp.bfloat16)

        return [functools.partial(part, r) for r in range(0, BLOCK, STRIP)]

    def grad_parts(step):
        (head, block), at, slot = steps[step], rows_of(step), step % 2

        def add(index, value):
            if block == 0:
                g_ref[index] = value
            else:
                g_ref[index] += value

        def part_q():
            g_ref[head * 3, at, :] = (
                jnp.dot(ds_ref[slot], x_ref[head * 4 + 1], preferred_element_type=jnp.float32) * scale
            )

        def part_k():
            add(head * 3 + 1, tn_dot(ds_ref[slot], x_ref[head * 4, at, :]) * scale)

        def part_v():
            add(head * 3 + 2, tn_dot(pl_ref[slot], e_ref[slot]))

        return [part_v, part_q, part_k]

    def weave(first, second):
        count = max(len(first), len(second))
        for i in range(count):
            for parts in (first, second):
                for part in parts[i * len(parts) // count : (i + 1) * len(parts) // count]:
                    part()

    zero = jnp.zeros((1, HD), jnp.float32)
    sums = (zero, zero)
    weave(score_parts(0), [])
    weave(soft_parts(0), [])
    for step in range(len(steps)):
        more = step + 1 < len(steps)
        sums = error_part(step, sums)
        weave(grad_prob_parts(step), [])
        weave(grad_score_parts(step), score_parts(step + 1) if more else [])
        weave(grad_parts(step), soft_parts(step + 1) if more else [])
    s0, s1 = sums

    parts = []
    for clip, (acc, count) in enumerate(zip((s0, s1), counts)):
        both = factor_ref[:, :HD] / (count * WIDTH)
        loss = jnp.sum(acc, axis=1, keepdims=True) * both
        parts.append((loss, loss * factor_ref[:, (1 + clip) * HD : (2 + clip) * HD] * both))
    lane_row = lax.broadcasted_iota(jnp.int32, (1, HD), 1)

    def spread(value, first):
        high, mid, rest = split3(value)
        return jnp.where(
            lane_row == first,
            high,
            jnp.where(lane_row == first + 1, mid, jnp.where(lane_row == first + 2, rest, 0.0)),
        )

    losses = spread(parts[0][0], 3) + spread(parts[1][0], 6)
    extra0 = losses + spread(parts[0][1], 0)
    extra1 = losses + spread(parts[1][1], 0)
    out_pair = 2 * OUT_PIECES * CAP

    def sort_out(i, carry):
        at = pl.ds(pl.multiple_of(i * 8, 8), 8)
        lab = lab_ref[at, :]
        tiles = [g_ref[j, at, :] for j in range(OUT_PIECES - 1)]
        tiles.append(jnp.where(lab == 0.0, extra0, jnp.where(lab == 1.0, extra1, losses)))
        turned = [swap(tile) for tile in tiles]
        first = [jnp.where(low, tiles[j], turned[j + 1]) for j in range(0, OUT_PIECES, 2)]
        second = [jnp.where(low, turned[j], tiles[j + 1]) for j in range(0, OUT_PIECES, 2)]
        base = pl.multiple_of(i * out_pair, out_pair)
        out_ref[pl.ds(base, out_pair), :] = jnp.concatenate(first + second, axis=0).astype(jnp.bfloat16)
        return carry

    loops = total // 8 // PARTS
    for part in range(PARTS):
        lax.fori_loop(part * loops, (part + 1) * loops, sort_out, 0, unroll=4)
        emit(part).start()
    for part in range(PARTS):
        emit(part).wait()


def attend(arrived, factors, sources):
    total = sources * CAP
    return pl.pallas_call(
        attend_kernel,
        in_specs=[pl.BlockSpec(memory_space=pltpu.VMEM)] * 2,
        out_specs=pl.BlockSpec(memory_space=pltpu.HBM),
        out_shape=jax.ShapeDtypeStruct((sources * OUT_PIECES * CAP, HD), jnp.bfloat16),
        scratch_shapes=[
            pltpu.VMEM((sources * OUT_PIECES * CAP, HD), jnp.bfloat16),
            pltpu.VMEM((12, total, HD), jnp.bfloat16),
            pltpu.VMEM((total, HD), jnp.float32),
            pltpu.VMEM((total, HD), jnp.bfloat16),
            pltpu.VMEM((total, HD), jnp.bfloat16),
            pltpu.VMEM((9, total, HD), jnp.float32),
            pltpu.VMEM((2, BLOCK, total), jnp.float32),
            pltpu.VMEM((2, BLOCK, total), jnp.float32),
            pltpu.VMEM((2, BLOCK, total), jnp.float32),
            pltpu.VMEM((2, BLOCK, total), jnp.bfloat16),
            pltpu.VMEM((2, BLOCK, total), jnp.bfloat16),
            pltpu.VMEM((2, BLOCK, HD), jnp.bfloat16),
            pltpu.SemaphoreType.DMA((PARTS,)),
        ],
        compiler_params=pltpu.CompilerParams(vmem_limit_bytes=VMEM_LIMIT),
        name="attend",
    )(arrived, factors)


def unpack_kernel(
    here_ref, in_ref, dq_ref, dk_ref, dv_ref, loss_ref, g_ref, out_sem, *, seq_size
):
    low = low_half()
    lane = lax.broadcasted_iota(jnp.int32, (8, HD), 1)
    tok_rows = dq_ref.shape[0]
    chunks = tok_rows // 16
    in_rows = in_ref.shape[0] // chunks
    stride = OUT_PIECES * CAP
    outs = (dq_ref, dk_ref, dv_ref)

    def emit(chunk, index):
        at = pl.ds(chunk * 16, 16)
        return pltpu.make_async_copy(g_ref.at[index, at], outs[index].at[at], out_sem.at[chunk, index])

    line = jnp.zeros((1, HD), jnp.float32)
    for chunk in range(chunks):
        block = in_ref[chunk * in_rows : (chunk + 1) * in_rows, :].astype(jnp.float32)

        def piece(tile, dest, j):
            even = ((tile * 2) * seq_size + dest) * stride + (j // 2) * 8
            odd = ((tile * 2 + 1) * seq_size + dest) * stride + (j // 2) * 8
            a, b = block[even : even + 8], block[odd : odd + 8]
            if j % 2 == 0:
                return jnp.where(low, a, swap(b))
            return jnp.where(low, swap(a), b)

        coefs = []
        for tile in range(2):
            extra = piece(tile, 0, OUT_PIECES - 1)
            for dest in range(1, seq_size):
                extra = extra + piece(tile, dest, OUT_PIECES - 1)
            coef = jnp.sum(jnp.where(lane < 3, extra, 0.0), axis=1, keepdims=True)
            coefs.append(jnp.broadcast_to(coef, (8, HD)))
            row = lax.broadcasted_iota(jnp.int32, (8, HD), 0)
            own = (here_ref[0] - chunk * 4 - tile * 2) * CAP
            line = line + jnp.sum(jnp.where(row == own, extra, 0.0), axis=0, keepdims=True)

        for index in range(3):
            for dest in range(seq_size):
                for head in range(3):
                    col = (dest * 3 + head) * HD
                    both = [piece(n, dest, head * 3 + index) * coefs[n] for n in range(2)]
                    g_ref[index, chunk * 16 : chunk * 16 + 16, col : col + HD] = jnp.concatenate(
                        both, axis=0
                    ).astype(jnp.bfloat16)
            emit(chunk, index).start()
    lane_row = lax.broadcasted_iota(jnp.int32, (1, HD), 1)
    for clip in range(CLIPS_G):
        mine = (lane_row >= 3 + 3 * clip) & (lane_row < 6 + 3 * clip)
        loss_ref[0:1, clip : clip + 1] = jnp.sum(jnp.where(mine, line, 0.0), axis=1, keepdims=True)
    for chunk in range(chunks):
        for index in range(3):
            emit(chunk, index).wait()


def unpack(returned, here, tok_rows, seq_size):
    chunks = tok_rows // 16
    width = seq_size * 3 * HD
    outside = pl.BlockSpec(memory_space=pltpu.HBM)
    grad_shape = jax.ShapeDtypeStruct((tok_rows, width), jnp.bfloat16)
    return pl.pallas_call(
        functools.partial(unpack_kernel, seq_size=seq_size),
        in_specs=[pl.BlockSpec(memory_space=pltpu.SMEM), pl.BlockSpec(memory_space=pltpu.VMEM)],
        out_specs=[outside] * 3 + [pl.BlockSpec(memory_space=pltpu.VMEM)],
        out_shape=[grad_shape] * 3 + [jax.ShapeDtypeStruct((1, CLIPS_G), jnp.float32)],
        scratch_shapes=[
            pltpu.VMEM((3, tok_rows, width), jnp.bfloat16),
            pltpu.SemaphoreType.DMA((chunks, 3)),
        ],
        compiler_params=pltpu.CompilerParams(vmem_limit_bytes=24 * 2**20),
        name="unpack",
    )(here, returned)


def shards(queries, key_rows, values, target, row_clip, ratios, ref_loss, noise_level):
    seq_size = lax.axis_size("seq")
    devices = lax.axis_size("dp") * seq_size
    tok_rows = queries.shape[0]
    sent = pack(queries, key_rows, values, target, row_clip.reshape(1, tok_rows))
    sent = sent.reshape(devices * IN_PIECES, CAP, HD)
    arrived = lax.all_to_all(sent, ("dp", "seq"), split_axis=0, concat_axis=0, tiled=True)
    arrived = arrived.reshape(devices * IN_PIECES * CAP, HD)
    weight_level = level_weight(noise_level)
    step = ratios / ref_loss * (2.0 * LOSS_SCALE)
    factors = jnp.concatenate(
        [jnp.broadcast_to(weight_level, (1, HD))]
        + [jnp.broadcast_to(step[:, c : c + 1], (1, HD)) for c in range(CLIPS_G)],
        axis=1,
    )
    grads = attend(arrived, factors, devices)
    grads = grads.reshape(devices, OUT_PIECES * CAP, HD)
    returned = lax.all_to_all(grads, ("dp", "seq"), split_axis=0, concat_axis=0, tiled=True)
    returned = returned.reshape(devices * OUT_PIECES * CAP, HD)
    here = lax.axis_index("dp").reshape(1).astype(jnp.int32)
    return tuple(unpack(returned, here, tok_rows, seq_size))


def solution(mesh):
    placed = (
        P(("dp", "seq"), None),
        P(("dp", "seq"), None),
        P(("dp", "seq"), None),
        P(("dp", "seq"), None),
        P(("dp", "seq")),
        P("dp", None),
        P("dp", None),
        P(),
    )
    return jax.shard_map(
        shards,
        mesh=mesh,
        in_specs=placed,
        out_specs=(
            P(("dp", "seq"), None),
            P(("dp", "seq"), None),
            P(("dp", "seq"), None),
            P("dp", None),
        ),
        check_vma=False,
    )
```

```python
import functools

import jax
import jax.numpy as jnp
from jax import lax
from jax.experimental import pallas as pl
from jax.experimental.pallas import tpu as pltpu
from jax.sharding import PartitionSpec as P

HEADS = 24
HD = 128
CLIPS_G = 2
LEVELS = 1000

SHIFT_FACTOR = 5.0
LOSS_SCALE = 2.0**21
MASK_FILL = 1e30
LOG2E = 1.4426950408889634
WIDTH = HEADS * HD

CAP = 4
TAIL = 2
IN_PIECES = 12
OUT_PIECES = 9
IN_ROWS = IN_PIECES * CAP + TAIL
OUT_ROWS = OUT_PIECES * CAP + TAIL
BLOCK = 512
STRIP = 32
NCUT = 256
PARTS = 8
ATTEND_LIMIT = 40 * 2**20
PACK_LIMIT = 61 * 2**20


def level_weight(noise_level):
    fraction = 1.0 - noise_level[0].astype(jnp.float32) / LEVELS
    sigma = SHIFT_FACTOR * fraction / (1.0 + (SHIFT_FACTOR - 1.0) * fraction)
    return 1.0 / (sigma * sigma + (1.0 - sigma) * (1.0 - sigma))


def row_iota():
    return lax.broadcasted_iota(jnp.int32, (8, HD), 0)


def shift(tile, by):
    return pltpu.roll(tile, by % 8, 0) if by % 8 else tile


def lay(pieces):
    row = row_iota()
    tiles, current, at = [], None, 0
    for tile, first, rows in pieces:
        moved = shift(tile, at - first)
        current = moved if at == 0 else jnp.where(row < at, current, moved)
        at += rows
        if at >= 8:
            tiles.append(current)
            current, at = moved, at - 8
    return tiles


def find(block, row):
    index, first = divmod(row, 8)
    tile = block[index * 8 : index * 8 + 8]
    if first <= 4:
        return tile, first
    return jnp.where(row_iota() < 4, block[index * 8 + 8 : index * 8 + 16], tile), first


def join(block, row, other):
    upper, first = find(block, row)
    lower, second = find(block, other)
    return jnp.where(row_iota() < 4, shift(upper, -first), shift(lower, 4 - second))


def pack_kernel(q_ref, k_ref, v_ref, t_ref, clip_ref, out_ref, x_ref, c_ref, lab_ref, o_ref, in_sem, clip_sem, out_sem):
    tok_rows, width = q_ref.shape
    seq_size = width // (3 * HD)
    chunks = tok_rows // 16
    out_rows = o_ref.shape[0] // chunks

    def fetch(chunk, tensor):
        at = pl.ds(chunk * 16, 16)
        ref = (q_ref, k_ref, v_ref, t_ref)[tensor]
        return pltpu.make_async_copy(ref.at[at], x_ref.at[tensor, at], in_sem.at[chunk, tensor])

    def emit(chunk):
        at = pl.ds(chunk * out_rows, out_rows)
        return pltpu.make_async_copy(o_ref.at[at], out_ref.at[at], out_sem.at[chunk])

    clip_copy = pltpu.make_async_copy(clip_ref, c_ref, clip_sem.at[0])
    clip_copy.start()
    for chunk in range(chunks):
        for tensor in range(4):
            fetch(chunk, tensor).start()
    clip_copy.wait()
    row = lax.broadcasted_iota(jnp.int32, (tok_rows, tok_rows), 0)
    lane = lax.broadcasted_iota(jnp.int32, (tok_rows, tok_rows), 1)
    clips = jnp.broadcast_to(c_ref[...].astype(jnp.float32), (tok_rows, tok_rows))
    labels = jnp.sum(jnp.where(row == lane, clips, 0.0), axis=1, keepdims=True)
    lab_ref[...] = jnp.broadcast_to(labels, (tok_rows, HD))
    front = lax.broadcasted_iota(jnp.int32, (8, HD), 1) < HD // 2
    for chunk in range(chunks):
        for tensor in range(4):
            fetch(chunk, tensor).wait()
        at = slice(chunk * 16, chunk * 16 + 16)
        tensors = [x_ref[tensor, at, :].astype(jnp.float32) for tensor in range(4)]
        for tile in range(2):
            eight = slice(tile * 8, tile * 8 + 8)
            label_tile = lab_ref[chunk * 16 + tile * 8 : chunk * 16 + tile * 8 + 8, :]
            label_tile = jnp.where(front, label_tile, shift(label_tile, -2))
            for half in range(2):
                made = []
                for dest in range(seq_size):
                    for head in range(3):
                        col = (dest * 3 + head) * HD
                        made.extend((tensor[eight, col : col + HD], half * CAP, CAP) for tensor in tensors)
                    made.append((label_tile, half * CAP, TAIL))
                count = seq_size * IN_ROWS
                start = ((chunk * 2 + tile) * 2 + half) * count
                o_ref[start : start + count, :] = jnp.concatenate(lay(made), axis=0).astype(jnp.bfloat16)
        emit(chunk).start()
    for chunk in range(chunks):
        emit(chunk).wait()


def pack(queries, key_rows, values, target, clip_row):
    tok_rows, width = queries.shape
    chunks = tok_rows // 16
    out_rows = tok_rows // CAP * (width // (3 * HD)) * IN_ROWS
    return pl.pallas_call(
        pack_kernel,
        in_specs=[pl.BlockSpec(memory_space=pltpu.HBM)] * 5,
        out_specs=pl.BlockSpec(memory_space=pltpu.HBM),
        out_shape=jax.ShapeDtypeStruct((out_rows, HD), jnp.bfloat16),
        scratch_shapes=[
            pltpu.VMEM((4, tok_rows, width), jnp.bfloat16),
            pltpu.VMEM((1, tok_rows), jnp.int32),
            pltpu.VMEM((tok_rows, HD), jnp.float32),
            pltpu.VMEM((out_rows, HD), jnp.bfloat16),
            pltpu.SemaphoreType.DMA((chunks, 4)),
            pltpu.SemaphoreType.DMA((1,)),
            pltpu.SemaphoreType.DMA((chunks,)),
        ],
        compiler_params=pltpu.CompilerParams(vmem_limit_bytes=PACK_LIMIT),
        name="pack",
    )(queries, key_rows, values, target, clip_row)


def split3(value):
    high = value.astype(jnp.bfloat16).astype(jnp.float32)
    rest = value - high
    mid = rest.astype(jnp.bfloat16).astype(jnp.float32)
    return high, mid, rest - mid


def nt_dot(a, b):
    return lax.dot_general(a, b, (((1,), (1,)), ((), ())), preferred_element_type=jnp.float32)


def tn_dot(a, b):
    return lax.dot_general(a, b, (((0,), (0,)), ((), ())), preferred_element_type=jnp.float32)


def attend_kernel(
    in_ref, factor_ref, sent_ref, out_ref, x_ref, lab_ref, fq_ref, fk_ref, g_ref,
    s_ref, p_ref, dp_ref, pl_ref, ds_ref, e_ref, out_sem,
):
    total = x_ref.shape[1]
    row = row_iota()
    front = lax.broadcasted_iota(jnp.int32, (8, HD), 1) < HD // 2
    out_part = out_ref.shape[0] // PARTS

    def emit(part):
        at = pl.ds(part * out_part, out_part)
        return pltpu.make_async_copy(out_ref.at[at], sent_ref.at[at], out_sem.at[part])


    def sort_in(i, carry):
        base = pl.multiple_of(i * (8 * IN_ROWS), 8 * IN_ROWS)
        block = in_ref[pl.ds(base, 8 * IN_ROWS), :].astype(jnp.float32)
        at = pl.ds(pl.multiple_of(i * 32, 32), 32)
        for j in range(IN_PIECES):
            start = j * CAP
            tiles = [join(block, 2 * u * IN_ROWS + start, (2 * u + 1) * IN_ROWS + start) for u in range(4)]
            x_ref[j, at, :] = jnp.concatenate(tiles, axis=0).astype(jnp.bfloat16)
        labels = []
        for u in range(4):
            start, other = 2 * u * IN_ROWS + IN_PIECES * CAP, (2 * u + 1) * IN_ROWS + IN_PIECES * CAP
            upper = shift(block[start // 8 * 8 : start // 8 * 8 + 8], -start)
            lower = shift(block[other // 8 * 8 : other // 8 * 8 + 8], 4 - other)
            tile = jnp.where(row < 4, upper, lower)
            turned = pltpu.roll(tile, HD // 2, 1)
            labels.append(
                jnp.where(
                    row % 4 < 2,
                    jnp.where(front, tile, turned),
                    shift(jnp.where(front, turned, tile), 2),
                )
            )
        lab_ref[at, :] = jnp.concatenate(labels, axis=0)
        return carry

    lax.fori_loop(0, total // 32, sort_in, 0, unroll=4)

    label = lab_ref[...]
    lane = lax.broadcasted_iota(jnp.int32, (total, HD), 1)
    is0 = jnp.where(label == 0.0, 1.0, 0.0)
    is1 = jnp.where(label == 1.0, 1.0, 0.0)
    empty = jnp.where(label < 0.0, 1.0, 0.0)
    fk_ref[...] = jnp.where(
        lane == 0, is0, jnp.where(lane == 1, is1, jnp.where(lane == 2, empty, 0.0))
    ).astype(jnp.bfloat16)
    fq_ref[...] = jnp.where(
        lane == 0,
        (is0 - 1.0) * MASK_FILL,
        jnp.where(lane == 1, (is1 - 1.0) * MASK_FILL, jnp.where(lane == 2, -MASK_FILL, 0.0)),
    ).astype(jnp.bfloat16)
    counts = (jnp.sum(is0, axis=0, keepdims=True), jnp.sum(is1, axis=0, keepdims=True))

    scale = HD**-0.5

    steps = [(head, block) for head in range(3) for block in range(total // BLOCK)]

    def rows_of(step):
        return slice(steps[step][1] * BLOCK, (steps[step][1] + 1) * BLOCK)

    def score_parts(step):
        head, at, slot = steps[step][0], rows_of(step), step % 2

        def part(n):
            cols = slice(n, n + NCUT)
            key_wide = jnp.concatenate([x_ref[head * 4 + 1, cols, :], fk_ref[cols, :]], axis=1)
            query_wide = jnp.concatenate([x_ref[head * 4, at, :], fq_ref[at, :]], axis=1)
            s_ref[slot, :, cols] = nt_dot(query_wide, key_wide)

        return [functools.partial(part, n) for n in range(0, total, NCUT)]

    def soft_parts(step):
        slot = step % 2

        def part(r):
            rows = slice(r, r + STRIP)
            scores = s_ref[slot, rows, :]
            largest = jnp.max(scores, axis=1, keepdims=True)
            expo = jnp.exp2((scores - largest) * (scale * LOG2E))
            probs = expo * (1.0 / jnp.sum(expo, axis=1, keepdims=True))
            p_ref[slot, rows, :] = probs
            pl_ref[slot, rows, :] = probs.astype(jnp.bfloat16)

        return [functools.partial(part, r) for r in range(0, BLOCK, STRIP)]

    def error_part(step, sums):
        head, at, slot = steps[step][0], rows_of(step), step % 2
        s0, s1 = sums
        output = jnp.dot(pl_ref[slot], x_ref[head * 4 + 2], preferred_element_type=jnp.float32)
        error = output - x_ref[head * 4 + 3, at, :].astype(jnp.float32)
        lab = lab_ref[at, :]
        error = jnp.where(lab >= 0.0, error, 0.0)
        square = error * error
        s0 = s0 + jnp.sum(jnp.where(lab == 0.0, square, 0.0), axis=0, keepdims=True)
        s1 = s1 + jnp.sum(jnp.where(lab == 1.0, square, 0.0), axis=0, keepdims=True)
        e_ref[slot] = error.astype(jnp.bfloat16)
        return s0, s1

    def grad_prob_parts(step):
        head, slot = steps[step][0], step % 2

        def part(n):
            cols = slice(n, n + NCUT)
            dp_ref[slot, :, cols] = nt_dot(e_ref[slot], x_ref[head * 4 + 2, cols, :])

        return [functools.partial(part, n) for n in range(0, total, NCUT)]

    def grad_score_parts(step):
        slot = step % 2

        def part(r):
            rows = slice(r, r + STRIP)
            grad_probs = dp_ref[slot, rows, :]
            probs = p_ref[slot, rows, :]
            inner = jnp.sum(probs * grad_probs, axis=1, keepdims=True)
            ds_ref[slot, rows, :] = (probs * (grad_probs - inner)).astype(jnp.bfloat16)

        return [functools.partial(part, r) for r in range(0, BLOCK, STRIP)]

    def grad_parts(step):
        (head, block), at, slot = steps[step], rows_of(step), step % 2

        def add(index, value):
            if block == 0:
                g_ref[index] = value
            else:
                g_ref[index] += value

        def part_q():
            g_ref[head * 3, at, :] = (
                jnp.dot(ds_ref[slot], x_ref[head * 4 + 1], preferred_element_type=jnp.float32) * scale
            )

        def part_k():
            add(head * 3 + 1, tn_dot(ds_ref[slot], x_ref[head * 4, at, :]) * scale)

        def part_v():
            add(head * 3 + 2, tn_dot(pl_ref[slot], e_ref[slot]))

        return [part_v, part_q, part_k]

    def weave(first, second):
        count = max(len(first), len(second))
        for i in range(count):
            for parts in (first, second):
                for part in parts[i * len(parts) // count : (i + 1) * len(parts) // count]:
                    part()

    zero = jnp.zeros((1, HD), jnp.float32)
    sums = (zero, zero)
    weave(score_parts(0), [])
    weave(soft_parts(0), [])
    for step in range(len(steps)):
        more = step + 1 < len(steps)
        sums = error_part(step, sums)
        weave(grad_prob_parts(step), [])
        weave(grad_score_parts(step), score_parts(step + 1) if more else [])
        weave(grad_parts(step), soft_parts(step + 1) if more else [])
    s0, s1 = sums

    parts = []
    for clip, (acc, count) in enumerate(zip((s0, s1), counts)):
        both = factor_ref[:, :HD] / (count * WIDTH)
        loss = jnp.sum(acc, axis=1, keepdims=True) * both
        parts.append((loss, loss * factor_ref[:, (1 + clip) * HD : (2 + clip) * HD] * both))
    lane_row = lax.broadcasted_iota(jnp.int32, (1, HD), 1)

    def spread(value, first):
        high, mid, rest = split3(value)
        return jnp.where(
            lane_row == first,
            high,
            jnp.where(lane_row == first + 1, mid, jnp.where(lane_row == first + 2, rest, 0.0)),
        )

    losses = spread(parts[0][0], 3) + spread(parts[1][0], 6)
    first0, first1 = spread(parts[0][1], 0), spread(parts[1][1], 0)
    later0, later1 = spread(parts[0][1], HD // 2), spread(parts[1][1], HD // 2)

    def sort_out(i, carry):
        at = pl.ds(pl.multiple_of(i * 32, 32), 32)
        grads = [g_ref[j, at, :] for j in range(OUT_PIECES)]
        labs = lab_ref[at, :]
        pieces = []
        for u in range(4):
            eight = slice(u * 8, u * 8 + 8)
            lab = labs[eight]
            tail = losses + jnp.where(lab == 0.0, first0, jnp.where(lab == 1.0, first1, 0.0))
            later = jnp.where(lab == 0.0, later0, jnp.where(lab == 1.0, later1, 0.0))
            tail = tail + shift(later, -2)
            for half in range(2):
                pieces.extend((grad[eight], half * CAP, CAP) for grad in grads)
                pieces.append((tail, half * CAP, TAIL))
        base = pl.multiple_of(i * (8 * OUT_ROWS), 8 * OUT_ROWS)
        out_ref[pl.ds(base, 8 * OUT_ROWS), :] = jnp.concatenate(lay(pieces), axis=0).astype(jnp.bfloat16)
        return carry

    loops = total // 32 // PARTS
    for part in range(PARTS):
        lax.fori_loop(part * loops, (part + 1) * loops, sort_out, 0, unroll=True)
        emit(part).start()
    for part in range(PARTS):
        emit(part).wait()


def attend(arrived, factors, sources):
    total = sources * CAP
    return pl.pallas_call(
        attend_kernel,
        in_specs=[pl.BlockSpec(memory_space=pltpu.VMEM)] * 2,
        out_specs=pl.BlockSpec(memory_space=pltpu.HBM),
        out_shape=pltpu.HBM((sources * OUT_ROWS, HD), jnp.bfloat16),
        scratch_shapes=[
            pltpu.VMEM((sources * OUT_ROWS, HD), jnp.bfloat16),
            pltpu.VMEM((12, total, HD), jnp.bfloat16),
            pltpu.VMEM((total, HD), jnp.float32),
            pltpu.VMEM((total, HD), jnp.bfloat16),
            pltpu.VMEM((total, HD), jnp.bfloat16),
            pltpu.VMEM((9, total, HD), jnp.float32),
            pltpu.VMEM((2, BLOCK, total), jnp.float32),
            pltpu.VMEM((2, BLOCK, total), jnp.float32),
            pltpu.VMEM((2, BLOCK, total), jnp.float32),
            pltpu.VMEM((2, BLOCK, total), jnp.bfloat16),
            pltpu.VMEM((2, BLOCK, total), jnp.bfloat16),
            pltpu.VMEM((2, BLOCK, HD), jnp.bfloat16),
            pltpu.SemaphoreType.DMA((PARTS,)),
        ],
        compiler_params=pltpu.CompilerParams(vmem_limit_bytes=ATTEND_LIMIT),
        name="attend",
    )(arrived, factors)


def unpack_kernel(
    here_ref, in_ref, dq_ref, dk_ref, dv_ref, loss_ref, g_ref, out_sem, *, seq_size
):
    row = row_iota()
    lane = lax.broadcasted_iota(jnp.int32, (8, HD), 1)
    tok_rows = dq_ref.shape[0]
    chunks = tok_rows // 16
    in_rows = in_ref.shape[0] // chunks
    outs = (dq_ref, dk_ref, dv_ref)

    def emit(chunk, index):
        at = pl.ds(chunk * 16, 16)
        return pltpu.make_async_copy(g_ref.at[index, at], outs[index].at[at], out_sem.at[chunk, index])

    line = jnp.zeros((1, HD), jnp.float32)
    for chunk in range(chunks):
        block = in_ref[chunk * in_rows : (chunk + 1) * in_rows, :].astype(jnp.float32)

        def starts(tile, dest):
            return [((tile * 2 + n) * seq_size + dest) * OUT_ROWS for n in range(2)]

        coefs = []
        for tile in range(2):
            extra = None
            for dest in range(seq_size):
                start, other = [first + OUT_PIECES * CAP for first in starts(tile, dest)]
                upper = shift(block[start // 8 * 8 : start // 8 * 8 + 8], -start)
                lower = shift(block[other // 8 * 8 : other // 8 * 8 + 8], 4 - other)
                one = jnp.where(row < 4, upper, lower)
                extra = one if extra is None else extra + one
            early = jnp.sum(jnp.where(lane < 3, extra, 0.0), axis=1, keepdims=True)
            late = jnp.where((lane >= HD // 2) & (lane < HD // 2 + 3), extra, 0.0)
            late = jnp.sum(late, axis=1, keepdims=True)
            late = shift(jnp.broadcast_to(late, (8, HD)), 2)
            coefs.append(jnp.where(row % 4 < 2, jnp.broadcast_to(early, (8, HD)), late))
            own = (here_ref[0] - chunk * 4 - tile * 2) * CAP
            line = line + jnp.sum(jnp.where(row == own, extra, 0.0), axis=0, keepdims=True)
        for index in range(3):
            for dest in range(seq_size):
                for head in range(3):
                    col = (dest * 3 + head) * HD
                    both = []
                    for tile in range(2):
                        start, other = [first + (head * 3 + index) * CAP for first in starts(tile, dest)]
                        both.append(join(block, start, other) * coefs[tile])
                    g_ref[index, chunk * 16 : chunk * 16 + 16, col : col + HD] = jnp.concatenate(
                        both, axis=0
                    ).astype(jnp.bfloat16)
            emit(chunk, index).start()
    lane_row = lax.broadcasted_iota(jnp.int32, (1, HD), 1)
    for clip in range(CLIPS_G):
        mine = (lane_row >= 3 + 3 * clip) & (lane_row < 6 + 3 * clip)
        loss_ref[0:1, clip : clip + 1] = jnp.sum(jnp.where(mine, line, 0.0), axis=1, keepdims=True)
    for chunk in range(chunks):
        for index in range(3):
            emit(chunk, index).wait()


def unpack(returned, here, tok_rows, seq_size):
    chunks = tok_rows // 16
    width = seq_size * 3 * HD
    outside = pl.BlockSpec(memory_space=pltpu.HBM)
    grad_shape = jax.ShapeDtypeStruct((tok_rows, width), jnp.bfloat16)
    return pl.pallas_call(
        functools.partial(unpack_kernel, seq_size=seq_size),
        in_specs=[pl.BlockSpec(memory_space=pltpu.SMEM), pl.BlockSpec(memory_space=pltpu.VMEM)],
        out_specs=[outside] * 3 + [pl.BlockSpec(memory_space=pltpu.VMEM)],
        out_shape=[grad_shape] * 3 + [jax.ShapeDtypeStruct((1, CLIPS_G), jnp.float32)],
        scratch_shapes=[
            pltpu.VMEM((3, tok_rows, width), jnp.bfloat16),
            pltpu.SemaphoreType.DMA((chunks, 3)),
        ],
        compiler_params=pltpu.CompilerParams(vmem_limit_bytes=24 * 2**20),
        name="unpack",
    )(here, returned)


def shards(queries, key_rows, values, target, row_clip, ratios, ref_loss, noise_level):
    seq_size = lax.axis_size("seq")
    devices = lax.axis_size("dp") * seq_size
    tok_rows = queries.shape[0]
    sent = pack(queries, key_rows, values, target, row_clip.reshape(1, tok_rows))
    sent = sent.reshape(devices * IN_ROWS // TAIL, TAIL, HD)
    arrived = lax.all_to_all(sent, ("dp", "seq"), split_axis=0, concat_axis=0, tiled=True)
    arrived = arrived.reshape(devices * IN_ROWS, HD)
    weight_level = level_weight(noise_level)
    step = ratios / ref_loss * (2.0 * LOSS_SCALE)
    factors = jnp.concatenate(
        [jnp.broadcast_to(weight_level, (1, HD))]
        + [jnp.broadcast_to(step[:, c : c + 1], (1, HD)) for c in range(CLIPS_G)],
        axis=1,
    )
    grads = attend(arrived, factors, devices)
    grads = grads.reshape(devices * OUT_ROWS // TAIL, TAIL, HD)
    returned = lax.all_to_all(grads, ("dp", "seq"), split_axis=0, concat_axis=0, tiled=True)
    returned = returned.reshape(devices * OUT_ROWS, HD)
    here = lax.axis_index("dp").reshape(1).astype(jnp.int32)
    return tuple(unpack(returned, here, tok_rows, seq_size))


def solution(mesh):
    placed = (
        P(("dp", "seq"), None),
        P(("dp", "seq"), None),
        P(("dp", "seq"), None),
        P(("dp", "seq"), None),
        P(("dp", "seq")),
        P("dp", None),
        P("dp", None),
        P(),
    )
    return jax.shard_map(
        shards,
        mesh=mesh,
        in_specs=placed,
        out_specs=(
            P(("dp", "seq"), None),
            P(("dp", "seq"), None),
            P(("dp", "seq"), None),
            P("dp", None),
        ),
        check_vma=False,
    )
```

```python
import functools

import jax
import jax.numpy as jnp
from jax import lax
from jax.experimental import pallas as pl
from jax.experimental.pallas import tpu as pltpu
from jax.sharding import PartitionSpec as P

HEADS = 24
HD = 128
CLIPS_G = 2
LEVELS = 1000

SHIFT_FACTOR = 5.0
LOSS_SCALE = 2.0**21
MASK_FILL = 1e30
LOG2E = 1.4426950408889634
WIDTH = HEADS * HD

Z_SIZE = 8
CAP = 4
TAIL = 2
IN_PIECES = 8
OUT_PIECES = 9
IN_ROWS = IN_PIECES * CAP + TAIL
OUT_ROWS = OUT_PIECES * CAP + TAIL
BLOCK = 512
STRIP = 32
NCUT = 256
PARTS = 8
ATTEND_LIMIT = 40 * 2**20
PACK_LIMIT = 61 * 2**20


def level_weight(noise_level):
    fraction = 1.0 - noise_level[0].astype(jnp.float32) / LEVELS
    sigma = SHIFT_FACTOR * fraction / (1.0 + (SHIFT_FACTOR - 1.0) * fraction)
    return 1.0 / (sigma * sigma + (1.0 - sigma) * (1.0 - sigma))


def row_iota():
    return lax.broadcasted_iota(jnp.int32, (8, HD), 0)


def shift(tile, by):
    return pltpu.roll(tile, by % 8, 0) if by % 8 else tile


def lay(pieces):
    row = row_iota()
    tiles, current, at = [], None, 0
    for tile, first, rows in pieces:
        moved = shift(tile, at - first)
        current = moved if at == 0 else jnp.where(row < at, current, moved)
        at += rows
        if at >= 8:
            tiles.append(current)
            current, at = moved, at - 8
    return tiles


def find(block, row):
    index, first = divmod(row, 8)
    tile = block[index * 8 : index * 8 + 8]
    if first <= 4:
        return tile, first
    return jnp.where(row_iota() < 4, block[index * 8 + 8 : index * 8 + 16], tile), first


def join(block, row, other):
    upper, first = find(block, row)
    lower, second = find(block, other)
    return jnp.where(row_iota() < 4, shift(upper, -first), shift(lower, 4 - second))


def pack_kernel(
    q_ref, k_ref, v_ref, t_ref, clip_ref, out_ref, third_ref, x_ref, c_ref, lab_ref, o_ref, third,
    in_sem, clip_sem, out_sem, third_sem,
):
    tok_rows, width = q_ref.shape
    seq_size = width // (3 * HD)
    chunks = tok_rows // 16
    groups = tok_rows // CAP
    out_rows = o_ref.shape[0] // chunks

    def fetch(chunk, tensor):
        at = pl.ds(chunk * 16, 16)
        ref = (q_ref, k_ref, v_ref, t_ref)[tensor]
        return pltpu.make_async_copy(ref.at[at], x_ref.at[tensor, at], in_sem.at[chunk, tensor])

    def emit(chunk):
        at = pl.ds(chunk * out_rows, out_rows)
        return pltpu.make_async_copy(o_ref.at[at], out_ref.at[at], out_sem.at[chunk])

    clip_copy = pltpu.make_async_copy(clip_ref, c_ref, clip_sem.at[0])
    clip_copy.start()
    for chunk in range(chunks):
        for tensor in range(4):
            fetch(chunk, tensor).start()
    clip_copy.wait()
    row = lax.broadcasted_iota(jnp.int32, (tok_rows, tok_rows), 0)
    lane = lax.broadcasted_iota(jnp.int32, (tok_rows, tok_rows), 1)
    clips = jnp.broadcast_to(c_ref[...].astype(jnp.float32), (tok_rows, tok_rows))
    labels = jnp.sum(jnp.where(row == lane, clips, 0.0), axis=1, keepdims=True)
    lab_ref[...] = jnp.broadcast_to(labels, (tok_rows, HD))
    front = lax.broadcasted_iota(jnp.int32, (8, HD), 1) < HD // 2
    for chunk in range(chunks):
        for tensor in range(4):
            fetch(chunk, tensor).wait()
        at = slice(chunk * 16, chunk * 16 + 16)
        tensors = [x_ref[tensor, at, :].astype(jnp.float32) for tensor in range(4)]
        for tile in range(2):
            eight = slice(tile * 8, tile * 8 + 8)
            label_tile = lab_ref[chunk * 16 + tile * 8 : chunk * 16 + tile * 8 + 8, :]
            label_tile = jnp.where(front, label_tile, shift(label_tile, -2))
            for dest in range(seq_size):
                col = (dest * 3 + 2) * HD
                for part in range(2):
                    pair = [tensor[eight, col : col + HD] for tensor in tensors[part * 2 : part * 2 + 2]]
                    both = [lay([(one, half * CAP, CAP) for one in pair])[0] for half in range(2)]
                    group = (chunk * 2 + tile) * 2
                    start = (((part * 2 + dest % 2) * (seq_size // 2) + dest // 2) * groups + group) * 8
                    third[start : start + 16, :] = jnp.concatenate(both, axis=0).astype(jnp.bfloat16)
            for half in range(2):
                made = []
                for dest in range(seq_size):
                    for head in range(2):
                        col = (dest * 3 + head) * HD
                        made.extend((tensor[eight, col : col + HD], half * CAP, CAP) for tensor in tensors)
                    made.append((label_tile, half * CAP, TAIL))
                count = seq_size * IN_ROWS
                start = ((chunk * 2 + tile) * 2 + half) * count
                o_ref[start : start + count, :] = jnp.concatenate(lay(made), axis=0).astype(jnp.bfloat16)
        emit(chunk).start()
    last_copy = pltpu.make_async_copy(third, third_ref, third_sem.at[0])
    last_copy.start()
    for chunk in range(chunks):
        emit(chunk).wait()
    last_copy.wait()


def pack(queries, key_rows, values, target, clip_row):
    tok_rows, width = queries.shape
    chunks = tok_rows // 16
    out_rows = tok_rows // CAP * (width // (3 * HD)) * IN_ROWS
    third_rows = tok_rows * 4 * (width // (3 * HD))
    return pl.pallas_call(
        pack_kernel,
        in_specs=[pl.BlockSpec(memory_space=pltpu.HBM)] * 5,
        out_specs=[pl.BlockSpec(memory_space=pltpu.HBM)] * 2,
        out_shape=[
            pltpu.HBM((out_rows, HD), jnp.bfloat16),
            pltpu.HBM((third_rows, HD), jnp.bfloat16),
        ],
        scratch_shapes=[
            pltpu.VMEM((4, tok_rows, width), jnp.bfloat16),
            pltpu.VMEM((1, tok_rows), jnp.int32),
            pltpu.VMEM((tok_rows, HD), jnp.float32),
            pltpu.VMEM((out_rows, HD), jnp.bfloat16),
            pltpu.VMEM((third_rows, HD), jnp.bfloat16),
            pltpu.SemaphoreType.DMA((chunks, 4)),
            pltpu.SemaphoreType.DMA((1,)),
            pltpu.SemaphoreType.DMA((chunks,)),
            pltpu.SemaphoreType.DMA((1,)),
        ],
        compiler_params=pltpu.CompilerParams(vmem_limit_bytes=PACK_LIMIT),
        name="pack",
    )(queries, key_rows, values, target, clip_row)


def split3(value):
    high = value.astype(jnp.bfloat16).astype(jnp.float32)
    rest = value - high
    mid = rest.astype(jnp.bfloat16).astype(jnp.float32)
    return high, mid, rest - mid


def nt_dot(a, b):
    return lax.dot_general(a, b, (((1,), (1,)), ((), ())), preferred_element_type=jnp.float32)


def tn_dot(a, b):
    return lax.dot_general(a, b, (((0,), (0,)), ((), ())), preferred_element_type=jnp.float32)


def run_heads(heads, sums, x_ref, lab_ref, fq_ref, fk_ref, g_ref, s_ref, p_ref, dp_ref, pl_ref, ds_ref, e_ref):
    total = x_ref.shape[1]
    scale = HD**-0.5
    label = lab_ref[...]
    lane = lax.broadcasted_iota(jnp.int32, (total, HD), 1)
    is0 = jnp.where(label == 0.0, 1.0, 0.0)
    is1 = jnp.where(label == 1.0, 1.0, 0.0)
    empty = jnp.where(label < 0.0, 1.0, 0.0)
    fk_ref[...] = jnp.where(
        lane == 0, is0, jnp.where(lane == 1, is1, jnp.where(lane == 2, empty, 0.0))
    ).astype(jnp.bfloat16)
    fq_ref[...] = jnp.where(
        lane == 0,
        (is0 - 1.0) * MASK_FILL,
        jnp.where(lane == 1, (is1 - 1.0) * MASK_FILL, jnp.where(lane == 2, -MASK_FILL, 0.0)),
    ).astype(jnp.bfloat16)

    steps = [(head, block) for head in range(heads) for block in range(total // BLOCK)]

    def rows_of(step):
        return slice(steps[step][1] * BLOCK, (steps[step][1] + 1) * BLOCK)

    def score_parts(step):
        head, at, slot = steps[step][0], rows_of(step), step % 2

        def part(n):
            cols = slice(n, n + NCUT)
            key_wide = jnp.concatenate([x_ref[head * 4 + 1, cols, :], fk_ref[cols, :]], axis=1)
            query_wide = jnp.concatenate([x_ref[head * 4, at, :], fq_ref[at, :]], axis=1)
            s_ref[slot, :, cols] = nt_dot(query_wide, key_wide)

        return [functools.partial(part, n) for n in range(0, total, NCUT)]

    def soft_parts(step):
        slot = step % 2

        def part(r):
            rows = slice(r, r + STRIP)
            scores = s_ref[slot, rows, :]
            largest = jnp.max(scores, axis=1, keepdims=True)
            expo = jnp.exp2((scores - largest) * (scale * LOG2E))
            probs = expo * (1.0 / jnp.sum(expo, axis=1, keepdims=True))
            p_ref[slot, rows, :] = probs
            pl_ref[slot, rows, :] = probs.astype(jnp.bfloat16)

        return [functools.partial(part, r) for r in range(0, BLOCK, STRIP)]

    def error_part(step, sums):
        head, at, slot = steps[step][0], rows_of(step), step % 2
        s0, s1 = sums
        output = jnp.dot(pl_ref[slot], x_ref[head * 4 + 2], preferred_element_type=jnp.float32)
        error = output - x_ref[head * 4 + 3, at, :].astype(jnp.float32)
        lab = lab_ref[at, :]
        error = jnp.where(lab >= 0.0, error, 0.0)
        square = error * error
        s0 = s0 + jnp.sum(jnp.where(lab == 0.0, square, 0.0), axis=0, keepdims=True)
        s1 = s1 + jnp.sum(jnp.where(lab == 1.0, square, 0.0), axis=0, keepdims=True)
        e_ref[slot] = error.astype(jnp.bfloat16)
        return s0, s1

    def grad_prob_parts(step):
        head, slot = steps[step][0], step % 2

        def part(n):
            cols = slice(n, n + NCUT)
            dp_ref[slot, :, cols] = nt_dot(e_ref[slot], x_ref[head * 4 + 2, cols, :])

        return [functools.partial(part, n) for n in range(0, total, NCUT)]

    def grad_score_parts(step):
        slot = step % 2

        def part(r):
            rows = slice(r, r + STRIP)
            grad_probs = dp_ref[slot, rows, :]
            probs = p_ref[slot, rows, :]
            inner = jnp.sum(probs * grad_probs, axis=1, keepdims=True)
            ds_ref[slot, rows, :] = (probs * (grad_probs - inner)).astype(jnp.bfloat16)

        return [functools.partial(part, r) for r in range(0, BLOCK, STRIP)]

    def grad_parts(step):
        (head, block), at, slot = steps[step], rows_of(step), step % 2

        def add(index, value):
            if block == 0:
                g_ref[index] = value
            else:
                g_ref[index] += value

        def part_q():
            g_ref[head * 3, at, :] = (
                jnp.dot(ds_ref[slot], x_ref[head * 4 + 1], preferred_element_type=jnp.float32) * scale
            )

        def part_k():
            add(head * 3 + 1, tn_dot(ds_ref[slot], x_ref[head * 4, at, :]) * scale)

        def part_v():
            add(head * 3 + 2, tn_dot(pl_ref[slot], e_ref[slot]))

        return [part_v, part_q, part_k]

    def weave(first, second):
        count = max(len(first), len(second))
        for i in range(count):
            for parts in (first, second):
                for part in parts[i * len(parts) // count : (i + 1) * len(parts) // count]:
                    part()

    weave(score_parts(0), [])
    weave(soft_parts(0), [])
    for step in range(len(steps)):
        more = step + 1 < len(steps)
        sums = error_part(step, sums)
        weave(grad_prob_parts(step), [])
        weave(grad_score_parts(step), score_parts(step + 1) if more else [])
        weave(grad_parts(step), soft_parts(step + 1) if more else [])
    return sums


def first_kernel(
    in_ref, g_out, lab_ref, sums_ref, x_ref, fq_ref, fk_ref, g_ref, *scratch
):
    total = x_ref.shape[1]
    row = row_iota()
    front = lax.broadcasted_iota(jnp.int32, (8, HD), 1) < HD // 2

    def sort_in(i, carry):
        base = pl.multiple_of(i * (8 * IN_ROWS), 8 * IN_ROWS)
        block = in_ref[pl.ds(base, 8 * IN_ROWS), :].astype(jnp.float32)
        at = pl.ds(pl.multiple_of(i * 32, 32), 32)
        for j in range(IN_PIECES):
            start = j * CAP
            tiles = [join(block, 2 * u * IN_ROWS + start, (2 * u + 1) * IN_ROWS + start) for u in range(4)]
            x_ref[j, at, :] = jnp.concatenate(tiles, axis=0).astype(jnp.bfloat16)
        labels = []
        for u in range(4):
            start, other = 2 * u * IN_ROWS + IN_PIECES * CAP, (2 * u + 1) * IN_ROWS + IN_PIECES * CAP
            upper = shift(block[start // 8 * 8 : start // 8 * 8 + 8], -start)
            lower = shift(block[other // 8 * 8 : other // 8 * 8 + 8], 4 - other)
            tile = jnp.where(row < 4, upper, lower)
            turned = pltpu.roll(tile, HD // 2, 1)
            labels.append(
                jnp.where(
                    row % 4 < 2,
                    jnp.where(front, tile, turned),
                    shift(jnp.where(front, turned, tile), 2),
                )
            )
        lab_ref[at, :] = jnp.concatenate(labels, axis=0)
        return carry

    lax.fori_loop(0, total // 32, sort_in, 0, unroll=4)
    zero = jnp.zeros((1, HD), jnp.float32)
    s0, s1 = run_heads(2, (zero, zero), x_ref, lab_ref, fq_ref, fk_ref, g_ref, *scratch)
    sums_ref[...] = jnp.where(row == 0, s0, jnp.where(row == 1, s1, 0.0))
    for j in range(6):
        g_out[j] = g_ref[j].astype(jnp.bfloat16)


def last_kernel(
    here_ref, g_in, lab_ref, sums_ref, factor_ref, *refs, z_size
):
    block_refs = refs[:z_size]
    sent_ref, out_ref, x_ref, fq_ref, fk_ref, g_ref = refs[z_size : z_size + 6]
    scratch, out_sem = refs[z_size + 6 : -1], refs[-1]
    total = x_ref.shape[1]
    out_part = out_ref.shape[0] // PARTS

    def emit(part):
        at = pl.ds(part * out_part, out_part)
        return pltpu.make_async_copy(out_ref.at[at], sent_ref.at[at], out_sem.at[part])

    row = row_iota()
    z_here, x_here, y_here, c_here = (here_ref[i] for i in range(4))
    y_odd, y_high, core_one = y_here % 2 == 1, y_here >= 2, c_here == 1
    for k, block_ref in enumerate(block_refs):
        block = block_ref[...].astype(jnp.float32)
        for kx in range(4):
            place = lax.bitwise_xor(x_here, kx) * z_size + lax.bitwise_xor(z_here, k)
            at = pl.ds(pl.multiple_of(place * 32, 32), 32)
            for part in range(2):
                made = []
                for ky in range(4):
                    tiles = []
                    for kc in range(2):
                        start = (((part * 2 + kc) * 4 + ky) * 4 + kx) * 8
                        tiles.append(block[start : start + 8])
                    made.append(
                        (jnp.where(core_one, tiles[1], tiles[0]), jnp.where(core_one, tiles[0], tiles[1]))
                    )
                for bit, flag in ((1, y_odd), (2, y_high)):
                    made = [
                        tuple(jnp.where(flag, made[i ^ bit][n], made[i][n]) for n in range(2)) for i in range(4)
                    ]
                upper = [jnp.where(row < CAP, one, shift(two, CAP)) for one, two in made]
                lower = [jnp.where(row < CAP, shift(one, CAP), two) for one, two in made]
                x_ref[part * 2, at, :] = jnp.concatenate(upper, axis=0).astype(jnp.bfloat16)
                x_ref[part * 2 + 1, at, :] = jnp.concatenate(lower, axis=0).astype(jnp.bfloat16)

    sums = (sums_ref[0:1, :], sums_ref[1:2, :])
    s0, s1 = run_heads(1, sums, x_ref, lab_ref, fq_ref, fk_ref, g_ref, *scratch)
    label = lab_ref[...]
    counts = tuple(
        jnp.sum(jnp.where(label == clip, 1.0, 0.0), axis=0, keepdims=True) for clip in (0.0, 1.0)
    )
    parts = []
    for clip, (acc, count) in enumerate(zip((s0, s1), counts)):
        both = factor_ref[:, :HD] / (count * WIDTH)
        loss = jnp.sum(acc, axis=1, keepdims=True) * both
        parts.append((loss, loss * factor_ref[:, (1 + clip) * HD : (2 + clip) * HD] * both))
    lane_row = lax.broadcasted_iota(jnp.int32, (1, HD), 1)

    def spread(value, first):
        high, mid, rest = split3(value)
        return jnp.where(
            lane_row == first,
            high,
            jnp.where(lane_row == first + 1, mid, jnp.where(lane_row == first + 2, rest, 0.0)),
        )

    losses = spread(parts[0][0], 3) + spread(parts[1][0], 6)
    first0, first1 = spread(parts[0][1], 0), spread(parts[1][1], 0)
    later0, later1 = spread(parts[0][1], HD // 2), spread(parts[1][1], HD // 2)

    def sort_out(i, carry):
        at = pl.ds(pl.multiple_of(i * 32, 32), 32)
        grads = [g_in[j, at, :].astype(jnp.float32) for j in range(6)]
        grads += [g_ref[j, at, :] for j in range(3)]
        labs = lab_ref[at, :]
        pieces = []
        for u in range(4):
            eight = slice(u * 8, u * 8 + 8)
            lab = labs[eight]
            tail = losses + jnp.where(lab == 0.0, first0, jnp.where(lab == 1.0, first1, 0.0))
            later = jnp.where(lab == 0.0, later0, jnp.where(lab == 1.0, later1, 0.0))
            tail = tail + shift(later, -2)
            for half in range(2):
                pieces.extend((grad[eight], half * CAP, CAP) for grad in grads)
                pieces.append((tail, half * CAP, TAIL))
        base = pl.multiple_of(i * (8 * OUT_ROWS), 8 * OUT_ROWS)
        out_ref[pl.ds(base, 8 * OUT_ROWS), :] = jnp.concatenate(lay(pieces), axis=0).astype(jnp.bfloat16)
        return carry

    loops = total // 32 // PARTS
    for part in range(PARTS):
        lax.fori_loop(part * loops, (part + 1) * loops, sort_out, 0, unroll=True)
        emit(part).start()
    for part in range(PARTS):
        emit(part).wait()


def scratch_of(heads, total):
    return [
        pltpu.VMEM((4 * heads, total, HD), jnp.bfloat16),
        pltpu.VMEM((total, HD), jnp.bfloat16),
        pltpu.VMEM((total, HD), jnp.bfloat16),
        pltpu.VMEM((3 * heads, total, HD), jnp.float32),
        pltpu.VMEM((2, BLOCK, total), jnp.float32),
        pltpu.VMEM((2, BLOCK, total), jnp.float32),
        pltpu.VMEM((2, BLOCK, total), jnp.float32),
        pltpu.VMEM((2, BLOCK, total), jnp.bfloat16),
        pltpu.VMEM((2, BLOCK, total), jnp.bfloat16),
        pltpu.VMEM((2, BLOCK, HD), jnp.bfloat16),
    ]


def attend_first(arrived, sources):
    total = sources * CAP
    inside = pl.BlockSpec(memory_space=pltpu.VMEM)
    return pl.pallas_call(
        first_kernel,
        in_specs=[inside],
        out_specs=[inside] * 3,
        out_shape=[
            jax.ShapeDtypeStruct((6, total, HD), jnp.bfloat16),
            jax.ShapeDtypeStruct((total, HD), jnp.float32),
            jax.ShapeDtypeStruct((8, HD), jnp.float32),
        ],
        scratch_shapes=scratch_of(2, total),
        compiler_params=pltpu.CompilerParams(vmem_limit_bytes=ATTEND_LIMIT),
        cost_estimate=pl.CostEstimate(flops=2 * 12 * total * total * HD, bytes_accessed=2**23, transcendentals=2 * total * total),
        name="attend_first",
    )(arrived)


def attend_last(grads, labels, sums, factors, blocks, here, sources):
    total = sources * CAP
    inside = pl.BlockSpec(memory_space=pltpu.VMEM)
    return pl.pallas_call(
        functools.partial(last_kernel, z_size=len(blocks)),
        in_specs=[pl.BlockSpec(memory_space=pltpu.SMEM)] + [inside] * (4 + len(blocks)),
        out_specs=pl.BlockSpec(memory_space=pltpu.HBM),
        out_shape=pltpu.HBM((sources * OUT_ROWS, HD), jnp.bfloat16),
        scratch_shapes=[pltpu.VMEM((sources * OUT_ROWS, HD), jnp.bfloat16)]
        + scratch_of(1, total)
        + [pltpu.SemaphoreType.DMA((PARTS,))],
        compiler_params=pltpu.CompilerParams(vmem_limit_bytes=ATTEND_LIMIT),
        cost_estimate=pl.CostEstimate(flops=12 * total * total * HD, bytes_accessed=2**23, transcendentals=total * total),
        name="attend_last",
    )(here, grads, labels, sums, factors, *blocks)


def unpack_kernel(
    here_ref, in_ref, dq_ref, dk_ref, dv_ref, loss_ref, g_ref, out_sem, *, seq_size
):
    row = row_iota()
    lane = lax.broadcasted_iota(jnp.int32, (8, HD), 1)
    tok_rows = dq_ref.shape[0]
    chunks = tok_rows // 16
    in_rows = in_ref.shape[0] // chunks
    outs = (dq_ref, dk_ref, dv_ref)

    def emit(chunk, index):
        at = pl.ds(chunk * 16, 16)
        return pltpu.make_async_copy(g_ref.at[index, at], outs[index].at[at], out_sem.at[chunk, index])

    line = jnp.zeros((1, HD), jnp.float32)
    for chunk in range(chunks):
        block = in_ref[chunk * in_rows : (chunk + 1) * in_rows, :].astype(jnp.float32)

        def starts(tile, dest):
            return [((tile * 2 + n) * seq_size + dest) * OUT_ROWS for n in range(2)]

        coefs = []
        for tile in range(2):
            extra = None
            for dest in range(seq_size):
                start, other = [first + OUT_PIECES * CAP for first in starts(tile, dest)]
                upper = shift(block[start // 8 * 8 : start // 8 * 8 + 8], -start)
                lower = shift(block[other // 8 * 8 : other // 8 * 8 + 8], 4 - other)
                one = jnp.where(row < 4, upper, lower)
                extra = one if extra is None else extra + one
            early = jnp.sum(jnp.where(lane < 3, extra, 0.0), axis=1, keepdims=True)
            late = jnp.where((lane >= HD // 2) & (lane < HD // 2 + 3), extra, 0.0)
            late = jnp.sum(late, axis=1, keepdims=True)
            late = shift(jnp.broadcast_to(late, (8, HD)), 2)
            coefs.append(jnp.where(row % 4 < 2, jnp.broadcast_to(early, (8, HD)), late))
            own = (here_ref[0] - chunk * 4 - tile * 2) * CAP
            line = line + jnp.sum(jnp.where(row == own, extra, 0.0), axis=0, keepdims=True)
        for index in range(3):
            for dest in range(seq_size):
                for head in range(3):
                    col = (dest * 3 + head) * HD
                    both = []
                    for tile in range(2):
                        start, other = [first + (head * 3 + index) * CAP for first in starts(tile, dest)]
                        both.append(join(block, start, other) * coefs[tile])
                    g_ref[index, chunk * 16 : chunk * 16 + 16, col : col + HD] = jnp.concatenate(
                        both, axis=0
                    ).astype(jnp.bfloat16)
            emit(chunk, index).start()
    lane_row = lax.broadcasted_iota(jnp.int32, (1, HD), 1)
    for clip in range(CLIPS_G):
        mine = (lane_row >= 3 + 3 * clip) & (lane_row < 6 + 3 * clip)
        loss_ref[0:1, clip : clip + 1] = jnp.sum(jnp.where(mine, line, 0.0), axis=1, keepdims=True)
    for chunk in range(chunks):
        for index in range(3):
            emit(chunk, index).wait()


def unpack(returned, here, tok_rows, seq_size):
    chunks = tok_rows // 16
    width = seq_size * 3 * HD
    outside = pl.BlockSpec(memory_space=pltpu.HBM)
    grad_shape = jax.ShapeDtypeStruct((tok_rows, width), jnp.bfloat16)
    return pl.pallas_call(
        functools.partial(unpack_kernel, seq_size=seq_size),
        in_specs=[pl.BlockSpec(memory_space=pltpu.SMEM), pl.BlockSpec(memory_space=pltpu.VMEM)],
        out_specs=[outside] * 3 + [pl.BlockSpec(memory_space=pltpu.VMEM)],
        out_shape=[grad_shape] * 3 + [jax.ShapeDtypeStruct((1, CLIPS_G), jnp.float32)],
        scratch_shapes=[
            pltpu.VMEM((3, tok_rows, width), jnp.bfloat16),
            pltpu.SemaphoreType.DMA((chunks, 3)),
        ],
        compiler_params=pltpu.CompilerParams(vmem_limit_bytes=24 * 2**20),
        name="unpack",
    )(here, returned)


def pick(array, index, dim):
    return lax.dynamic_slice_in_dim(array, index, 1, dim)


def spread_third(third, seq_size, groups):
    s_here, d_here = lax.axis_index("seq"), lax.axis_index("dp")
    c_here, y_here = lax.rem(s_here, 2), lax.div(s_here, 2)
    x_here, z_here = lax.div(d_here, Z_SIZE), lax.rem(d_here, Z_SIZE)
    y_size, x_size = seq_size // 2, groups // Z_SIZE
    xor = lax.bitwise_xor

    def send(array, axis, distance, whole):
        return lax.ppermute(array, axis, [(i, i ^ distance) for i in range(whole)])

    array = third.reshape(2, 2, y_size, x_size, Z_SIZE, 8, HD)
    other = send(pick(array, xor(c_here, 1), 1), "seq", 1, seq_size)
    array = jnp.concatenate([pick(array, c_here, 1), other], axis=1)

    def both_ways(first, second):
        outs = [pick(first, xor(y_here, k), 1) for k in range(y_size)]
        outs += [pick(second, xor(x_here, k), 2) for k in range(x_size)]
        outs = lax.optimization_barrier(outs)
        came = [send(out, "seq", 2 * k, seq_size) if k else out for k, out in enumerate(outs[:y_size])]
        came += [send(out, "dp", Z_SIZE * k, groups) if k else out for k, out in enumerate(outs[y_size:])]
        came = lax.optimization_barrier(came)
        return jnp.concatenate(came[:y_size], axis=1), jnp.concatenate(came[y_size:], axis=2)

    front, back = both_ways(array[0], array[1])
    back, front = both_ways(back, front)
    array = jnp.stack([front, back])
    outs = [pick(array, xor(z_here, k), 4).reshape(-1, HD) for k in range(Z_SIZE)]
    outs = lax.optimization_barrier(outs)
    return [send(out, "dp", k, groups) if k > 1 else out for k, out in enumerate(outs)]


def shards(queries, key_rows, values, target, row_clip, ratios, ref_loss, noise_level):
    seq_size = lax.axis_size("seq")
    devices = lax.axis_size("dp") * seq_size
    tok_rows = queries.shape[0]
    sent, third = pack(queries, key_rows, values, target, row_clip.reshape(1, tok_rows))
    sent = sent.reshape(devices * IN_ROWS // TAIL, TAIL, HD)
    arrived = lax.all_to_all(sent, ("dp", "seq"), split_axis=0, concat_axis=0, tiled=True)
    arrived = arrived.reshape(devices * IN_ROWS, HD)
    blocks = spread_third(third, seq_size, devices // seq_size)
    weight_level = level_weight(noise_level)
    step = ratios / ref_loss * (2.0 * LOSS_SCALE)
    factors = jnp.concatenate(
        [jnp.broadcast_to(weight_level, (1, HD))]
        + [jnp.broadcast_to(step[:, c : c + 1], (1, HD)) for c in range(CLIPS_G)],
        axis=1,
    )
    first = attend_first(arrived, devices)
    near, first = lax.optimization_barrier((blocks[1], first))
    blocks[1] = lax.ppermute(near, "dp", [(i, i ^ 1) for i in range(devices // seq_size)])
    s_here, d_here = lax.axis_index("seq"), lax.axis_index("dp")
    places = (lax.rem(d_here, Z_SIZE), lax.div(d_here, Z_SIZE), lax.div(s_here, 2), lax.rem(s_here, 2))
    places = jnp.stack([place.astype(jnp.int32) for place in places])
    grads = attend_last(*first, factors, blocks, places, devices)
    grads = grads.reshape(devices * OUT_ROWS // TAIL, TAIL, HD)
    returned = lax.all_to_all(grads, ("dp", "seq"), split_axis=0, concat_axis=0, tiled=True)
    returned = returned.reshape(devices * OUT_ROWS, HD)
    here = lax.axis_index("dp").reshape(1).astype(jnp.int32)
    return tuple(unpack(returned, here, tok_rows, seq_size))


def solution(mesh):
    placed = (
        P(("dp", "seq"), None),
        P(("dp", "seq"), None),
        P(("dp", "seq"), None),
        P(("dp", "seq"), None),
        P(("dp", "seq")),
        P("dp", None),
        P("dp", None),
        P(),
    )
    return jax.shard_map(
        shards,
        mesh=mesh,
        in_specs=placed,
        out_specs=(
            P(("dp", "seq"), None),
            P(("dp", "seq"), None),
            P(("dp", "seq"), None),
            P("dp", None),
        ),
        check_vma=False,
    )
```

```python
import functools

import jax
import jax.numpy as jnp
from jax import lax
from jax.experimental import pallas as pl
from jax.experimental.pallas import tpu as pltpu
from jax.sharding import PartitionSpec as P

HEADS = 24
HD = 128
CLIPS_G = 2
LEVELS = 1000

SHIFT_FACTOR = 5.0
LOSS_SCALE = 2.0**21
MASK_FILL = 1e30
LOG2E = 1.4426950408889634
WIDTH = HEADS * HD

Z_SIZE = 8
CAP = 4
TAIL = 2
IN_PIECES = 8
OUT_PIECES = 3
FIRST_ROWS = 6 * CAP
IN_ROWS = IN_PIECES * CAP + TAIL
OUT_ROWS = OUT_PIECES * CAP + TAIL
BLOCK = 512
STRIP = 32
NCUT = 256
PARTS = 8
ATTEND_LIMIT = 40 * 2**20
PACK_LIMIT = 61 * 2**20


def level_weight(noise_level):
    fraction = 1.0 - noise_level[0].astype(jnp.float32) / LEVELS
    sigma = SHIFT_FACTOR * fraction / (1.0 + (SHIFT_FACTOR - 1.0) * fraction)
    return 1.0 / (sigma * sigma + (1.0 - sigma) * (1.0 - sigma))


def row_iota():
    return lax.broadcasted_iota(jnp.int32, (8, HD), 0)


def shift(tile, by):
    return pltpu.roll(tile, by % 8, 0) if by % 8 else tile


def lay(pieces):
    row = row_iota()
    tiles, current, at = [], None, 0
    for tile, first, rows in pieces:
        moved = shift(tile, at - first)
        current = moved if at == 0 else jnp.where(row < at, current, moved)
        at += rows
        if at >= 8:
            tiles.append(current)
            current, at = moved, at - 8
    return tiles


def find(block, row):
    index, first = divmod(row, 8)
    tile = block[index * 8 : index * 8 + 8]
    if first <= 4:
        return tile, first
    return jnp.where(row_iota() < 4, block[index * 8 + 8 : index * 8 + 16], tile), first


def join(block, row, other):
    upper, first = find(block, row)
    lower, second = find(block, other)
    return jnp.where(row_iota() < 4, shift(upper, -first), shift(lower, 4 - second))


def pack_kernel(
    q_ref, k_ref, v_ref, t_ref, clip_ref, out_ref, third_ref, x_ref, c_ref, lab_ref, o_ref, third,
    in_sem, clip_sem, out_sem, third_sem,
):
    tok_rows, width = q_ref.shape
    seq_size = width // (3 * HD)
    chunks = tok_rows // 16
    groups = tok_rows // CAP
    out_rows = o_ref.shape[0] // chunks

    def fetch(chunk, tensor):
        at = pl.ds(chunk * 16, 16)
        ref = (q_ref, k_ref, v_ref, t_ref)[tensor]
        return pltpu.make_async_copy(ref.at[at], x_ref.at[tensor, at], in_sem.at[chunk, tensor])

    def emit(chunk):
        at = pl.ds(chunk * out_rows, out_rows)
        return pltpu.make_async_copy(o_ref.at[at], out_ref.at[at], out_sem.at[chunk])

    clip_copy = pltpu.make_async_copy(clip_ref, c_ref, clip_sem.at[0])
    clip_copy.start()
    for chunk in range(chunks):
        for tensor in range(4):
            fetch(chunk, tensor).start()
    clip_copy.wait()
    row = lax.broadcasted_iota(jnp.int32, (tok_rows, tok_rows), 0)
    lane = lax.broadcasted_iota(jnp.int32, (tok_rows, tok_rows), 1)
    clips = jnp.broadcast_to(c_ref[...].astype(jnp.float32), (tok_rows, tok_rows))
    labels = jnp.sum(jnp.where(row == lane, clips, 0.0), axis=1, keepdims=True)
    lab_ref[...] = jnp.broadcast_to(labels, (tok_rows, HD))
    front = lax.broadcasted_iota(jnp.int32, (8, HD), 1) < HD // 2
    for chunk in range(chunks):
        for tensor in range(4):
            fetch(chunk, tensor).wait()
        at = slice(chunk * 16, chunk * 16 + 16)
        tensors = [x_ref[tensor, at, :].astype(jnp.float32) for tensor in range(4)]
        for tile in range(2):
            eight = slice(tile * 8, tile * 8 + 8)
            label_tile = lab_ref[chunk * 16 + tile * 8 : chunk * 16 + tile * 8 + 8, :]
            label_tile = jnp.where(front, label_tile, shift(label_tile, -2))
            for dest in range(seq_size):
                col = (dest * 3 + 2) * HD
                for part in range(2):
                    pair = [tensor[eight, col : col + HD] for tensor in tensors[part * 2 : part * 2 + 2]]
                    both = [lay([(one, half * CAP, CAP) for one in pair])[0] for half in range(2)]
                    group = (chunk * 2 + tile) * 2
                    start = (((part * 2 + dest % 2) * (seq_size // 2) + dest // 2) * groups + group) * 8
                    third[start : start + 16, :] = jnp.concatenate(both, axis=0).astype(jnp.bfloat16)
            for half in range(2):
                made = []
                for dest in range(seq_size):
                    for head in range(2):
                        col = (dest * 3 + head) * HD
                        made.extend((tensor[eight, col : col + HD], half * CAP, CAP) for tensor in tensors)
                    made.append((label_tile, half * CAP, TAIL))
                count = seq_size * IN_ROWS
                start = ((chunk * 2 + tile) * 2 + half) * count
                o_ref[start : start + count, :] = jnp.concatenate(lay(made), axis=0).astype(jnp.bfloat16)
        emit(chunk).start()
    last_copy = pltpu.make_async_copy(third, third_ref, third_sem.at[0])
    last_copy.start()
    for chunk in range(chunks):
        emit(chunk).wait()
    last_copy.wait()


def pack(queries, key_rows, values, target, clip_row):
    tok_rows, width = queries.shape
    chunks = tok_rows // 16
    out_rows = tok_rows // CAP * (width // (3 * HD)) * IN_ROWS
    third_rows = tok_rows * 4 * (width // (3 * HD))
    return pl.pallas_call(
        pack_kernel,
        in_specs=[pl.BlockSpec(memory_space=pltpu.HBM)] * 5,
        out_specs=[pl.BlockSpec(memory_space=pltpu.HBM)] * 2,
        out_shape=[
            pltpu.HBM((out_rows, HD), jnp.bfloat16),
            pltpu.HBM((third_rows, HD), jnp.bfloat16),
        ],
        scratch_shapes=[
            pltpu.VMEM((4, tok_rows, width), jnp.bfloat16),
            pltpu.VMEM((1, tok_rows), jnp.int32),
            pltpu.VMEM((tok_rows, HD), jnp.float32),
            pltpu.VMEM((out_rows, HD), jnp.bfloat16),
            pltpu.VMEM((third_rows, HD), jnp.bfloat16),
            pltpu.SemaphoreType.DMA((chunks, 4)),
            pltpu.SemaphoreType.DMA((1,)),
            pltpu.SemaphoreType.DMA((chunks,)),
            pltpu.SemaphoreType.DMA((1,)),
        ],
        compiler_params=pltpu.CompilerParams(vmem_limit_bytes=PACK_LIMIT),
        name="pack",
    )(queries, key_rows, values, target, clip_row)


def split3(value):
    high = value.astype(jnp.bfloat16).astype(jnp.float32)
    rest = value - high
    mid = rest.astype(jnp.bfloat16).astype(jnp.float32)
    return high, mid, rest - mid


def nt_dot(a, b):
    return lax.dot_general(a, b, (((1,), (1,)), ((), ())), preferred_element_type=jnp.float32)


def tn_dot(a, b):
    return lax.dot_general(a, b, (((0,), (0,)), ((), ())), preferred_element_type=jnp.float32)


def run_heads(heads, sums, x_ref, lab_ref, fq_ref, fk_ref, g_ref, s_ref, p_ref, dp_ref, pl_ref, ds_ref, e_ref):
    total = x_ref.shape[1]
    scale = HD**-0.5
    label = lab_ref[...]
    lane = lax.broadcasted_iota(jnp.int32, (total, HD), 1)
    is0 = jnp.where(label == 0.0, 1.0, 0.0)
    is1 = jnp.where(label == 1.0, 1.0, 0.0)
    empty = jnp.where(label < 0.0, 1.0, 0.0)
    fk_ref[...] = jnp.where(
        lane == 0, is0, jnp.where(lane == 1, is1, jnp.where(lane == 2, empty, 0.0))
    ).astype(jnp.bfloat16)
    fq_ref[...] = jnp.where(
        lane == 0,
        (is0 - 1.0) * MASK_FILL,
        jnp.where(lane == 1, (is1 - 1.0) * MASK_FILL, jnp.where(lane == 2, -MASK_FILL, 0.0)),
    ).astype(jnp.bfloat16)

    steps = [(head, block) for head in range(heads) for block in range(total // BLOCK)]

    def rows_of(step):
        return slice(steps[step][1] * BLOCK, (steps[step][1] + 1) * BLOCK)

    def score_parts(step):
        head, at, slot = steps[step][0], rows_of(step), step % 2

        def part(n):
            cols = slice(n, n + NCUT)
            key_wide = jnp.concatenate([x_ref[head * 4 + 1, cols, :], fk_ref[cols, :]], axis=1)
            query_wide = jnp.concatenate([x_ref[head * 4, at, :], fq_ref[at, :]], axis=1)
            s_ref[slot, :, cols] = nt_dot(query_wide, key_wide)

        return [functools.partial(part, n) for n in range(0, total, NCUT)]

    def soft_parts(step):
        slot = step % 2

        def part(r):
            rows = slice(r, r + STRIP)
            scores = s_ref[slot, rows, :]
            largest = jnp.max(scores, axis=1, keepdims=True)
            expo = jnp.exp2((scores - largest) * (scale * LOG2E))
            probs = expo * (1.0 / jnp.sum(expo, axis=1, keepdims=True))
            p_ref[slot, rows, :] = probs
            pl_ref[slot, rows, :] = probs.astype(jnp.bfloat16)

        return [functools.partial(part, r) for r in range(0, BLOCK, STRIP)]

    def error_part(step, sums):
        head, at, slot = steps[step][0], rows_of(step), step % 2
        s0, s1 = sums
        output = jnp.dot(pl_ref[slot], x_ref[head * 4 + 2], preferred_element_type=jnp.float32)
        error = output - x_ref[head * 4 + 3, at, :].astype(jnp.float32)
        lab = lab_ref[at, :]
        error = jnp.where(lab >= 0.0, error, 0.0)
        square = error * error
        s0 = s0 + jnp.sum(jnp.where(lab == 0.0, square, 0.0), axis=0, keepdims=True)
        s1 = s1 + jnp.sum(jnp.where(lab == 1.0, square, 0.0), axis=0, keepdims=True)
        e_ref[slot] = error.astype(jnp.bfloat16)
        return s0, s1

    def grad_prob_parts(step):
        head, slot = steps[step][0], step % 2

        def part(n):
            cols = slice(n, n + NCUT)
            dp_ref[slot, :, cols] = nt_dot(e_ref[slot], x_ref[head * 4 + 2, cols, :])

        return [functools.partial(part, n) for n in range(0, total, NCUT)]

    def grad_score_parts(step):
        slot = step % 2

        def part(r):
            rows = slice(r, r + STRIP)
            grad_probs = dp_ref[slot, rows, :]
            probs = p_ref[slot, rows, :]
            inner = jnp.sum(probs * grad_probs, axis=1, keepdims=True)
            ds_ref[slot, rows, :] = (probs * (grad_probs - inner)).astype(jnp.bfloat16)

        return [functools.partial(part, r) for r in range(0, BLOCK, STRIP)]

    def grad_parts(step):
        (head, block), at, slot = steps[step], rows_of(step), step % 2

        def add(index, value):
            if block == 0:
                g_ref[index] = value
            else:
                g_ref[index] += value

        def part_q():
            g_ref[head * 3, at, :] = (
                jnp.dot(ds_ref[slot], x_ref[head * 4 + 1], preferred_element_type=jnp.float32) * scale
            )

        def part_k():
            add(head * 3 + 1, tn_dot(ds_ref[slot], x_ref[head * 4, at, :]) * scale)

        def part_v():
            add(head * 3 + 2, tn_dot(pl_ref[slot], e_ref[slot]))

        return [part_v, part_q, part_k]

    def weave(first, second):
        count = max(len(first), len(second))
        for i in range(count):
            for parts in (first, second):
                for part in parts[i * len(parts) // count : (i + 1) * len(parts) // count]:
                    part()

    weave(score_parts(0), [])
    weave(soft_parts(0), [])
    for step in range(len(steps)):
        more = step + 1 < len(steps)
        sums = error_part(step, sums)
        weave(grad_prob_parts(step), [])
        weave(grad_score_parts(step), score_parts(step + 1) if more else [])
        weave(grad_parts(step), soft_parts(step + 1) if more else [])
    return sums


def first_kernel(
    in_ref, sent_ref, lab_ref, sums_ref, out_ref, x_ref, fq_ref, fk_ref, g_ref, *refs
):
    scratch, out_sem = refs[:-1], refs[-1]
    total = x_ref.shape[1]
    out_part = out_ref.shape[0] // PARTS

    def emit(part):
        at = pl.ds(part * out_part, out_part)
        return pltpu.make_async_copy(out_ref.at[at], sent_ref.at[at], out_sem.at[part])

    row = row_iota()
    front = lax.broadcasted_iota(jnp.int32, (8, HD), 1) < HD // 2

    def sort_in(i, carry):
        base = pl.multiple_of(i * (8 * IN_ROWS), 8 * IN_ROWS)
        block = in_ref[pl.ds(base, 8 * IN_ROWS), :].astype(jnp.float32)
        at = pl.ds(pl.multiple_of(i * 32, 32), 32)
        for j in range(IN_PIECES):
            start = j * CAP
            tiles = [join(block, 2 * u * IN_ROWS + start, (2 * u + 1) * IN_ROWS + start) for u in range(4)]
            x_ref[j, at, :] = jnp.concatenate(tiles, axis=0).astype(jnp.bfloat16)
        labels = []
        for u in range(4):
            start, other = 2 * u * IN_ROWS + IN_PIECES * CAP, (2 * u + 1) * IN_ROWS + IN_PIECES * CAP
            upper = shift(block[start // 8 * 8 : start // 8 * 8 + 8], -start)
            lower = shift(block[other // 8 * 8 : other // 8 * 8 + 8], 4 - other)
            tile = jnp.where(row < 4, upper, lower)
            turned = pltpu.roll(tile, HD // 2, 1)
            labels.append(
                jnp.where(
                    row % 4 < 2,
                    jnp.where(front, tile, turned),
                    shift(jnp.where(front, turned, tile), 2),
                )
            )
        lab_ref[at, :] = jnp.concatenate(labels, axis=0)
        return carry

    lax.fori_loop(0, total // 32, sort_in, 0, unroll=4)
    zero = jnp.zeros((1, HD), jnp.float32)
    s0, s1 = run_heads(2, (zero, zero), x_ref, lab_ref, fq_ref, fk_ref, g_ref, *scratch)
    sums_ref[...] = jnp.where(row == 0, s0, jnp.where(row == 1, s1, 0.0))

    def sort_out(i, carry):
        at = pl.ds(pl.multiple_of(i * 32, 32), 32)
        grads = [g_ref[j, at, :] for j in range(6)]
        pieces = []
        for u in range(4):
            for half in range(2):
                pieces.extend((grad[u * 8 : u * 8 + 8], half * CAP, CAP) for grad in grads)
        base = pl.multiple_of(i * (8 * FIRST_ROWS), 8 * FIRST_ROWS)
        out_ref[pl.ds(base, 8 * FIRST_ROWS), :] = jnp.concatenate(lay(pieces), axis=0).astype(jnp.bfloat16)
        return carry

    loops = total // 32 // PARTS
    for part in range(PARTS):
        lax.fori_loop(part * loops, (part + 1) * loops, sort_out, 0, unroll=True)
        emit(part).start()
    for part in range(PARTS):
        emit(part).wait()


def last_kernel(
    here_ref, lab_ref, sums_ref, factor_ref, *refs, z_size
):
    block_refs = refs[:z_size]
    sent_ref, out_ref, x_ref, fq_ref, fk_ref, g_ref = refs[z_size : z_size + 6]
    scratch, out_sem = refs[z_size + 6 : -1], refs[-1]
    total = x_ref.shape[1]
    out_part = out_ref.shape[0] // PARTS

    def emit(part):
        at = pl.ds(part * out_part, out_part)
        return pltpu.make_async_copy(out_ref.at[at], sent_ref.at[at], out_sem.at[part])

    row = row_iota()
    z_here, x_here, y_here, c_here = (here_ref[i] for i in range(4))
    y_odd, y_high, core_one = y_here % 2 == 1, y_here >= 2, c_here == 1
    for k, block_ref in enumerate(block_refs):
        block = block_ref[...].astype(jnp.float32)
        for kx in range(4):
            place = lax.bitwise_xor(x_here, kx) * z_size + lax.bitwise_xor(z_here, k)
            at = pl.ds(pl.multiple_of(place * 32, 32), 32)
            for part in range(2):
                made = []
                for ky in range(4):
                    tiles = []
                    for kc in range(2):
                        start = (((part * 2 + kc) * 4 + ky) * 4 + kx) * 8
                        tiles.append(block[start : start + 8])
                    made.append(
                        (jnp.where(core_one, tiles[1], tiles[0]), jnp.where(core_one, tiles[0], tiles[1]))
                    )
                for bit, flag in ((1, y_odd), (2, y_high)):
                    made = [
                        tuple(jnp.where(flag, made[i ^ bit][n], made[i][n]) for n in range(2)) for i in range(4)
                    ]
                upper = [jnp.where(row < CAP, one, shift(two, CAP)) for one, two in made]
                lower = [jnp.where(row < CAP, shift(one, CAP), two) for one, two in made]
                x_ref[part * 2, at, :] = jnp.concatenate(upper, axis=0).astype(jnp.bfloat16)
                x_ref[part * 2 + 1, at, :] = jnp.concatenate(lower, axis=0).astype(jnp.bfloat16)

    sums = (sums_ref[0:1, :], sums_ref[1:2, :])
    s0, s1 = run_heads(1, sums, x_ref, lab_ref, fq_ref, fk_ref, g_ref, *scratch)
    label = lab_ref[...]
    counts = tuple(
        jnp.sum(jnp.where(label == clip, 1.0, 0.0), axis=0, keepdims=True) for clip in (0.0, 1.0)
    )
    parts = []
    for clip, (acc, count) in enumerate(zip((s0, s1), counts)):
        both = factor_ref[:, :HD] / (count * WIDTH)
        loss = jnp.sum(acc, axis=1, keepdims=True) * both
        parts.append((loss, loss * factor_ref[:, (1 + clip) * HD : (2 + clip) * HD] * both))
    lane_row = lax.broadcasted_iota(jnp.int32, (1, HD), 1)

    def spread(value, first):
        high, mid, rest = split3(value)
        return jnp.where(
            lane_row == first,
            high,
            jnp.where(lane_row == first + 1, mid, jnp.where(lane_row == first + 2, rest, 0.0)),
        )

    losses = spread(parts[0][0], 3) + spread(parts[1][0], 6)
    first0, first1 = spread(parts[0][1], 0), spread(parts[1][1], 0)
    later0, later1 = spread(parts[0][1], HD // 2), spread(parts[1][1], HD // 2)

    def sort_out(i, carry):
        at = pl.ds(pl.multiple_of(i * 32, 32), 32)
        grads = [g_ref[j, at, :] for j in range(OUT_PIECES)]
        labs = lab_ref[at, :]
        pieces = []
        for u in range(4):
            eight = slice(u * 8, u * 8 + 8)
            lab = labs[eight]
            tail = losses + jnp.where(lab == 0.0, first0, jnp.where(lab == 1.0, first1, 0.0))
            later = jnp.where(lab == 0.0, later0, jnp.where(lab == 1.0, later1, 0.0))
            tail = tail + shift(later, -2)
            for half in range(2):
                pieces.extend((grad[eight], half * CAP, CAP) for grad in grads)
                pieces.append((tail, half * CAP, TAIL))
        base = pl.multiple_of(i * (8 * OUT_ROWS), 8 * OUT_ROWS)
        out_ref[pl.ds(base, 8 * OUT_ROWS), :] = jnp.concatenate(lay(pieces), axis=0).astype(jnp.bfloat16)
        return carry

    loops = total // 32 // PARTS
    for part in range(PARTS):
        lax.fori_loop(part * loops, (part + 1) * loops, sort_out, 0, unroll=True)
        emit(part).start()
    for part in range(PARTS):
        emit(part).wait()


def scratch_of(heads, total):
    return [
        pltpu.VMEM((4 * heads, total, HD), jnp.bfloat16),
        pltpu.VMEM((total, HD), jnp.bfloat16),
        pltpu.VMEM((total, HD), jnp.bfloat16),
        pltpu.VMEM((3 * heads, total, HD), jnp.float32),
        pltpu.VMEM((2, BLOCK, total), jnp.float32),
        pltpu.VMEM((2, BLOCK, total), jnp.float32),
        pltpu.VMEM((2, BLOCK, total), jnp.float32),
        pltpu.VMEM((2, BLOCK, total), jnp.bfloat16),
        pltpu.VMEM((2, BLOCK, total), jnp.bfloat16),
        pltpu.VMEM((2, BLOCK, HD), jnp.bfloat16),
    ]


def attend_first(arrived, sources):
    total = sources * CAP
    inside = pl.BlockSpec(memory_space=pltpu.VMEM)
    return pl.pallas_call(
        first_kernel,
        in_specs=[inside],
        out_specs=[pl.BlockSpec(memory_space=pltpu.HBM)] + [inside] * 2,
        out_shape=[
            pltpu.HBM((sources * FIRST_ROWS, HD), jnp.bfloat16),
            jax.ShapeDtypeStruct((total, HD), jnp.float32),
            jax.ShapeDtypeStruct((8, HD), jnp.float32),
        ],
        scratch_shapes=[pltpu.VMEM((sources * FIRST_ROWS, HD), jnp.bfloat16)]
        + scratch_of(2, total)
        + [pltpu.SemaphoreType.DMA((PARTS,))],
        compiler_params=pltpu.CompilerParams(vmem_limit_bytes=ATTEND_LIMIT),
        cost_estimate=pl.CostEstimate(flops=2 * 12 * total * total * HD, bytes_accessed=2**23, transcendentals=2 * total * total),
        name="attend_first",
    )(arrived)


def attend_last(labels, sums, factors, blocks, here, sources):
    total = sources * CAP
    inside = pl.BlockSpec(memory_space=pltpu.VMEM)
    return pl.pallas_call(
        functools.partial(last_kernel, z_size=len(blocks)),
        in_specs=[pl.BlockSpec(memory_space=pltpu.SMEM)] + [inside] * (3 + len(blocks)),
        out_specs=pl.BlockSpec(memory_space=pltpu.HBM),
        out_shape=pltpu.HBM((sources * OUT_ROWS, HD), jnp.bfloat16),
        scratch_shapes=[pltpu.VMEM((sources * OUT_ROWS, HD), jnp.bfloat16)]
        + scratch_of(1, total)
        + [pltpu.SemaphoreType.DMA((PARTS,))],
        compiler_params=pltpu.CompilerParams(vmem_limit_bytes=ATTEND_LIMIT),
        cost_estimate=pl.CostEstimate(flops=12 * total * total * HD, bytes_accessed=2**23, transcendentals=total * total),
        name="attend_last",
    )(here, labels, sums, factors, *blocks)


def unpack_kernel(
    here_ref, first_ref, in_ref, dq_ref, dk_ref, dv_ref, loss_ref, g_ref, out_sem, *, seq_size
):
    row = row_iota()
    lane = lax.broadcasted_iota(jnp.int32, (8, HD), 1)
    tok_rows = dq_ref.shape[0]
    chunks = tok_rows // 16
    in_rows = in_ref.shape[0] // chunks
    first_rows = first_ref.shape[0] // chunks
    outs = (dq_ref, dk_ref, dv_ref)

    def emit(chunk, index):
        at = pl.ds(chunk * 16, 16)
        return pltpu.make_async_copy(g_ref.at[index, at], outs[index].at[at], out_sem.at[chunk, index])

    line = jnp.zeros((1, HD), jnp.float32)
    for chunk in range(chunks):
        block = in_ref[chunk * in_rows : (chunk + 1) * in_rows, :].astype(jnp.float32)
        first_block = first_ref[chunk * first_rows : (chunk + 1) * first_rows, :].astype(jnp.float32)

        def starts(tile, dest, rows):
            return [((tile * 2 + n) * seq_size + dest) * rows for n in range(2)]

        coefs = []
        for tile in range(2):
            extra = None
            for dest in range(seq_size):
                start, other = [first + OUT_PIECES * CAP for first in starts(tile, dest, OUT_ROWS)]
                upper = shift(block[start // 8 * 8 : start // 8 * 8 + 8], -start)
                lower = shift(block[other // 8 * 8 : other // 8 * 8 + 8], 4 - other)
                one = jnp.where(row < 4, upper, lower)
                extra = one if extra is None else extra + one
            early = jnp.sum(jnp.where(lane < 3, extra, 0.0), axis=1, keepdims=True)
            late = jnp.where((lane >= HD // 2) & (lane < HD // 2 + 3), extra, 0.0)
            late = jnp.sum(late, axis=1, keepdims=True)
            late = shift(jnp.broadcast_to(late, (8, HD)), 2)
            coefs.append(jnp.where(row % 4 < 2, jnp.broadcast_to(early, (8, HD)), late))
            own = (here_ref[0] - chunk * 4 - tile * 2) * CAP
            line = line + jnp.sum(jnp.where(row == own, extra, 0.0), axis=0, keepdims=True)
        for index in range(3):
            for dest in range(seq_size):
                for head in range(3):
                    col = (dest * 3 + head) * HD
                    both = []
                    for tile in range(2):
                        if head < 2:
                            rows = starts(tile, dest, FIRST_ROWS)
                            one = join(first_block, *[at + (head * 3 + index) * CAP for at in rows])
                        else:
                            rows = starts(tile, dest, OUT_ROWS)
                            one = join(block, *[at + index * CAP for at in rows])
                        both.append(one * coefs[tile])
                    g_ref[index, chunk * 16 : chunk * 16 + 16, col : col + HD] = jnp.concatenate(
                        both, axis=0
                    ).astype(jnp.bfloat16)
            emit(chunk, index).start()
    lane_row = lax.broadcasted_iota(jnp.int32, (1, HD), 1)
    for clip in range(CLIPS_G):
        mine = (lane_row >= 3 + 3 * clip) & (lane_row < 6 + 3 * clip)
        loss_ref[0:1, clip : clip + 1] = jnp.sum(jnp.where(mine, line, 0.0), axis=1, keepdims=True)
    for chunk in range(chunks):
        for index in range(3):
            emit(chunk, index).wait()


def unpack(first, returned, here, tok_rows, seq_size):
    chunks = tok_rows // 16
    width = seq_size * 3 * HD
    outside = pl.BlockSpec(memory_space=pltpu.HBM)
    grad_shape = jax.ShapeDtypeStruct((tok_rows, width), jnp.bfloat16)
    return pl.pallas_call(
        functools.partial(unpack_kernel, seq_size=seq_size),
        in_specs=[pl.BlockSpec(memory_space=pltpu.SMEM)] + [pl.BlockSpec(memory_space=pltpu.VMEM)] * 2,
        out_specs=[outside] * 3 + [pl.BlockSpec(memory_space=pltpu.VMEM)],
        out_shape=[grad_shape] * 3 + [jax.ShapeDtypeStruct((1, CLIPS_G), jnp.float32)],
        scratch_shapes=[
            pltpu.VMEM((3, tok_rows, width), jnp.bfloat16),
            pltpu.SemaphoreType.DMA((chunks, 3)),
        ],
        compiler_params=pltpu.CompilerParams(vmem_limit_bytes=24 * 2**20),
        name="unpack",
    )(here, first, returned)


def pick(array, index, dim):
    return lax.dynamic_slice_in_dim(array, index, 1, dim)


def spread_third(third, seq_size, groups):
    s_here, d_here = lax.axis_index("seq"), lax.axis_index("dp")
    c_here, y_here = lax.rem(s_here, 2), lax.div(s_here, 2)
    x_here, z_here = lax.div(d_here, Z_SIZE), lax.rem(d_here, Z_SIZE)
    y_size, x_size = seq_size // 2, groups // Z_SIZE
    xor = lax.bitwise_xor

    def send(array, axis, distance, whole):
        return lax.ppermute(array, axis, [(i, i ^ distance) for i in range(whole)])

    array = third.reshape(2, 2, y_size, x_size, Z_SIZE, 8, HD)
    other = send(pick(array, xor(c_here, 1), 1), "seq", 1, seq_size)
    array = jnp.concatenate([pick(array, c_here, 1), other], axis=1)

    def both_ways(first, second):
        outs = [pick(first, xor(y_here, k), 1) for k in range(y_size)]
        outs += [pick(second, xor(x_here, k), 2) for k in range(x_size)]
        outs = lax.optimization_barrier(outs)
        came = [send(out, "seq", 2 * k, seq_size) if k else out for k, out in enumerate(outs[:y_size])]
        came += [send(out, "dp", Z_SIZE * k, groups) if k else out for k, out in enumerate(outs[y_size:])]
        came = lax.optimization_barrier(came)
        return jnp.concatenate(came[:y_size], axis=1), jnp.concatenate(came[y_size:], axis=2)

    front, back = both_ways(array[0], array[1])
    back, front = both_ways(back, front)
    array = jnp.stack([front, back])
    outs = [pick(array, xor(z_here, k), 4).reshape(-1, HD) for k in range(Z_SIZE)]
    outs = lax.optimization_barrier(outs)
    return [send(out, "dp", k, groups) if k > 1 else out for k, out in enumerate(outs)]


def shards(queries, key_rows, values, target, row_clip, ratios, ref_loss, noise_level):
    seq_size = lax.axis_size("seq")
    devices = lax.axis_size("dp") * seq_size
    tok_rows = queries.shape[0]
    sent, third = pack(queries, key_rows, values, target, row_clip.reshape(1, tok_rows))
    sent = sent.reshape(devices * IN_ROWS // TAIL, TAIL, HD)
    arrived = lax.all_to_all(sent, ("dp", "seq"), split_axis=0, concat_axis=0, tiled=True)
    arrived = arrived.reshape(devices * IN_ROWS, HD)
    blocks = spread_third(third, seq_size, devices // seq_size)
    weight_level = level_weight(noise_level)
    step = ratios / ref_loss * (2.0 * LOSS_SCALE)
    factors = jnp.concatenate(
        [jnp.broadcast_to(weight_level, (1, HD))]
        + [jnp.broadcast_to(step[:, c : c + 1], (1, HD)) for c in range(CLIPS_G)],
        axis=1,
    )
    first, *labels_sums = attend_first(arrived, devices)
    near, first, labels_sums = lax.optimization_barrier((blocks[1], first, labels_sums))
    blocks[1] = lax.ppermute(near, "dp", [(i, i ^ 1) for i in range(devices // seq_size)])
    s_here, d_here = lax.axis_index("seq"), lax.axis_index("dp")
    places = (lax.rem(d_here, Z_SIZE), lax.div(d_here, Z_SIZE), lax.div(s_here, 2), lax.rem(s_here, 2))
    places = jnp.stack([place.astype(jnp.int32) for place in places])
    first = first.reshape(devices * FIRST_ROWS // CAP, CAP, HD)
    first = lax.all_to_all(first, ("dp", "seq"), split_axis=0, concat_axis=0, tiled=True)
    first = first.reshape(devices * FIRST_ROWS, HD)
    grads = attend_last(*labels_sums, factors, blocks, places, devices)
    first, grads = lax.optimization_barrier((first, grads))
    grads = grads.reshape(devices * OUT_ROWS // TAIL, TAIL, HD)
    returned = lax.all_to_all(grads, ("dp", "seq"), split_axis=0, concat_axis=0, tiled=True)
    returned = returned.reshape(devices * OUT_ROWS, HD)
    here = lax.axis_index("dp").reshape(1).astype(jnp.int32)
    return tuple(unpack(first, returned, here, tok_rows, seq_size))


def solution(mesh):
    placed = (
        P(("dp", "seq"), None),
        P(("dp", "seq"), None),
        P(("dp", "seq"), None),
        P(("dp", "seq"), None),
        P(("dp", "seq")),
        P("dp", None),
        P("dp", None),
        P(),
    )
    return jax.shard_map(
        shards,
        mesh=mesh,
        in_specs=placed,
        out_specs=(
            P(("dp", "seq"), None),
            P(("dp", "seq"), None),
            P(("dp", "seq"), None),
            P("dp", None),
        ),
        check_vma=False,
    )
```
